32 devices in a mesh: groups: 2 (over x), blk: 16 (over z, y, core).
Axes of the slice: x: 2, y: 2, z: 4, core: 2. Of those that a mesh axis runs over, the one named last changes fastest.
Arguments:
- queries: bfloat16 [4096, 512], P(('groups', 'blk')), parts along dimension 0, may hold values from -8 to 8
- key_states: bfloat16 [4096, 128], P(('groups', 'blk')), parts along dimension 0, may hold values from -6 to 6
- value_states: bfloat16 [4096, 128], P(('groups', 'blk')), parts along dimension 0, may hold values from -6 to 6
- grad_out: bfloat16 [4096, 512], P(('groups', 'blk')), parts along dimension 0, may hold values from -6 to 6
- tile_mask: int32 [32, 16], P('groups'), parts along dimension 0, may hold values 0 or 1
- block_order: int32 [32], P('groups'), parts along dimension 0, may hold values from 0 to 15, each once
Outputs:
- attended: bfloat16 [4096, 512], P(('groups', 'blk')), parts along dimension 0
- grad_queries: bfloat16 [4096, 512], P(('groups', 'blk')), parts along dimension 0
- grad_keys: float32 [4096, 128], P(('groups', 'blk')), parts along dimension 0
- grad_values: float32 [4096, 128], P(('groups', 'blk')), parts along dimension 0
The draws below stay inside these ranges and needn't reach their ends.
There are 2 independent parts, one for each index of `groups`. The reference program is written for one: setup_inputs(seed, part) draws one part's arguments, and reference() takes and returns one part's arrays. A program takes and returns all parts, laid end to end along the dimension named above; each array names one. Nothing has to cross between parts.
Inputs may be any that keep to these rules, and one draw needn't show every extreme that they name: `block_order`: each block number appears once.
All inputs are finite; a program needn't handle non-finite values.
Results may differ from the reference program's by a relative error of at most 0.04.
Values may be sent and summed in bfloat16 or wider, within the bound.
A program may use at most 64 MiB of HBM per device.

```python
import jax
import jax.numpy as jnp
from jax import lax

HD = 128
HEADS = 4
TILE = 128
TOK_DEV = 128
BLOCKS = 16
SEQ = 2048
NT = 16


def draw_queries(key, part):
    result = jnp.clip(jax.random.normal(jax.random.fold_in(key, 1), (SEQ, HEADS * HD), jnp.float32), -4.0, 4.0)
    return result.astype(jnp.bfloat16)


def draw_key_states(key, part):
    result = jnp.clip(jax.random.normal(jax.random.fold_in(key, 2), (SEQ, HD), jnp.float32), -4.0, 4.0)
    return result.astype(jnp.bfloat16)


def with_ends(array, rng, smallest, largest):
    index_at = [jax.random.randint(jax.random.fold_in(rng, axis), (), 0, length) for axis, length in enumerate(array.shape)]
    widest = array.shape.index(max(array.shape))
    neighbour = index_at[:widest] + [(index_at[widest] + 1) % array.shape[widest]] + index_at[widest + 1:]
    return array.at[tuple(index_at)].set(smallest).at[tuple(neighbour)].set(largest)


def steps_of(stream_key, extent, split, least, top_value):
    def one(position, blocks):
        heights = jax.random.uniform(jax.random.fold_in(jax.random.fold_in(stream_key, 6), position), (blocks,), jnp.float32, least / len(split), top_value / len(split))
        return jnp.repeat(jnp.exp(heights), extent[position] // blocks).reshape((-1,) + (1,) * (len(extent) - position - 1))

    factor_of = one(*split[0])
    for cut in split[1:]:
        factor_of = factor_of * one(*cut)
    return factor_of


def bell_draw(stream_key, dims, deviation, reach, cuts=(), held_as=jnp.bfloat16):
    level = steps_of(stream_key, dims, cuts, -0.22, 0.18) if cuts else 1.0
    values = jax.random.normal(stream_key, dims, jnp.float32) * deviation * level
    return jnp.minimum(jnp.maximum(values, -reach), reach).astype(held_as)


def setup_inputs(seed: int = 0, part: int = 0) -> dict:
    key_list = jax.random.split(jax.random.key(seed), 7)
    part_keys = jax.random.split(jax.random.fold_in(key_list[6], part), 7)
    queries = draw_queries(jax.random.fold_in(jax.random.fold_in(key_list[6], part), 71), part)
    key_states = draw_key_states(jax.random.fold_in(jax.random.fold_in(key_list[6], part), 71), part)
    value_states = bell_draw(part_keys[2], (SEQ, HD), 1.0, 6.0, ((0, 16),))
    grad_out = bell_draw(part_keys[3], (SEQ, HEADS * HD), 1.0, 6.0, ((0, 16),))
    tile_mask = with_ends((jax.random.randint(part_keys[4], (NT, NT), 0, 2) < 1).astype(jnp.int32), jax.random.fold_in(part_keys[4], 1), 0, 1)
    block_order = jax.random.permutation(part_keys[5], BLOCKS).astype(jnp.int32)
    return dict(queries=queries, key_states=key_states, value_states=value_states, grad_out=grad_out, tile_mask=tile_mask, block_order=block_order)


def token_positions(block_order):
    row_ids = jnp.arange(SEQ, dtype=jnp.int32)
    return (block_order[row_ids // TOK_DEV] * TOK_DEV + row_ids % TOK_DEV).astype(jnp.int32)


def reference(queries, key_states, value_states, grad_out, tile_mask, block_order):
    scaling = HD ** -0.5
    positions = token_positions(block_order)
    key_tiles = positions // TILE
    block_rows = min(512, SEQ)
    block_count = SEQ // block_rows

    def mask_for(start):
        query_pos = lax.dynamic_slice_in_dim(positions, start, block_rows)
        query_tiles = query_pos // TILE
        tile_bits = tile_mask[query_tiles[:, None], key_tiles[None, :]]
        same_tile = query_tiles[:, None] == key_tiles[None, :]
        return (query_pos[:, None] >= positions[None, :]) & ((tile_bits == 1) | same_tile)

    def forward_block(block_num):
        start = (block_num * block_rows).astype(jnp.int32)
        allowed = mask_for(start)
        query_block = lax.dynamic_slice_in_dim(queries, start, block_rows)
        outputs = []
        sums = []
        for head_num in range(HEADS):
            query_head = query_block[:, head_num * HD:(head_num + 1) * HD]
            scores = jnp.dot(query_head, key_states.T, preferred_element_type=jnp.float32) * scaling
            scores = jnp.where(allowed, scores, -jnp.inf)
            top_score = jnp.max(scores, axis=1)
            log_sum = top_score + jnp.log(jnp.sum(jnp.exp(scores - top_score[:, None]), axis=1))
            weights = jnp.exp(scores - log_sum[:, None]).astype(jnp.bfloat16)
            outputs.append(jnp.dot(weights, value_states, preferred_element_type=jnp.float32))
            sums.append(log_sum)
        return jnp.concatenate(outputs, axis=1).astype(jnp.bfloat16), jnp.stack(sums, axis=1)

    attended, log_sums = lax.map(forward_block, jnp.arange(block_count, dtype=jnp.int32))
    attended = attended.reshape(SEQ, HEADS * HD)
    log_sums = log_sums.reshape(SEQ, HEADS)

    def backward_block(carry_grads, block_num):
        grad_keys, grad_values = carry_grads
        start = (block_num * block_rows).astype(jnp.int32)
        allowed = mask_for(start)
        query_block = lax.dynamic_slice_in_dim(queries, start, block_rows)
        out_block = lax.dynamic_slice_in_dim(attended, start, block_rows)
        cot_block = lax.dynamic_slice_in_dim(grad_out, start, block_rows)
        sum_block = lax.dynamic_slice_in_dim(log_sums, start, block_rows)
        pieces = []
        for head_num in range(HEADS):
            cols = slice(head_num * HD, (head_num + 1) * HD)
            query_head = query_block[:, cols]
            cot_head = cot_block[:, cols]
            row_delta = jnp.sum(cot_head.astype(jnp.float32) * out_block[:, cols].astype(jnp.float32), axis=1)
            scores = jnp.dot(query_head, key_states.T, preferred_element_type=jnp.float32) * scaling
            scores = jnp.where(allowed, scores, -jnp.inf)
            weights = jnp.exp(scores - sum_block[:, head_num][:, None])
            grad_values = grad_values + jnp.dot(weights.astype(jnp.bfloat16).T, cot_head, preferred_element_type=jnp.float32)
            d_prob = jnp.dot(cot_head, value_states.T, preferred_element_type=jnp.float32)
            d_score = (weights * (d_prob - row_delta[:, None])).astype(jnp.bfloat16)
            pieces.append(jnp.dot(d_score, key_states, preferred_element_type=jnp.float32) * scaling)
            grad_keys = grad_keys + jnp.dot(d_score.T, query_head, preferred_element_type=jnp.float32) * scaling
        return (grad_keys, grad_values), jnp.concatenate(pieces, axis=1).astype(jnp.bfloat16)

    zero_grads = (jnp.zeros((SEQ, HD), jnp.float32), jnp.zeros((SEQ, HD), jnp.float32))
    (grad_keys, grad_values), grad_queries = lax.scan(backward_block, zero_grads, jnp.arange(block_count, dtype=jnp.int32))
    grad_queries = grad_queries.reshape(SEQ, HEADS * HD)
    return attended, grad_queries, grad_keys, grad_values
```

```python
import functools
import math

import jax
import jax.numpy as jnp
from jax import lax
from jax.experimental import pallas as pl
from jax.experimental.pallas import tpu as pltpu
from jax.sharding import PartitionSpec as P

MESH = pl.DeviceIdType.MESH
F32 = jnp.float32
BF16 = jnp.bfloat16
MASKED = -1e30


def dot(a, b):
    return jnp.dot(a, b, preferred_element_type=F32)


def dot_t(a, b):
    return lax.dot_general(a, b, (((1,), (1,)), ((), ())), preferred_element_type=F32)


def kernel(
    n, q_hbm, k_hbm, v_hbm, g_hbm, mask_hbm, order_hbm, att_ref, dq_ref, dk_ref, dv_ref,
    mask_ref, order_ref, q_ref, g_ref, kv, rt, prob, dprob, stat, mine, send_z, recv_z, send_c, recv_c, send_y, recv_y,
    in_s, z_s, z_r, y_s, y_r, c_s, c_r, f_s, f_r, t_s, t_r, gz_s, gz_r, gc_s, gc_r, gy_s, gy_r,
):
    m = n // 4
    tok, hd = k_hbm.shape
    heads = q_hbm.shape[1] // hd
    rows = heads * tok
    keys = m * tok
    scale = hd ** -0.5
    to_exp2 = scale * math.log2(math.e)
    KEY, VALUE = 0, 1
    QUERY, GRAD = 0, 1
    OUT, DQ = 0, 1
    OWN, SIBLING, DIAGONAL, PARTNER = 0, 1, 2, 3
    quad = (OWN, SIBLING, DIAGONAL, PARTNER)
    others = (DIAGONAL, PARTNER, SIBLING)

    me = lax.axis_index("blk")
    z, y, c = me // 4, (me // 2) % 2, me % 2

    def index(rz, j):
        zz = lax.rem(z + rz, m)
        yy = 1 - y if j & 2 else y
        cc = 1 - c if j & 1 else c
        return (zz * 2 + yy) * 2 + cc

    def chunk(rz):
        return index(rz, 1 if rz else 0)

    def remote(src, dst, s_sem, r_sem, target):
        return pltpu.make_async_remote_copy(
            src_ref=src, dst_ref=dst, send_sem=s_sem, recv_sem=r_sem,
            device_id={"blk": target}, device_id_type=MESH,
        )

    def gather_z(t, g):
        return remote(kv.at[t, 0], kv.at[t, m - g], z_s.at[t, g], z_r.at[t, m - g], chunk(g))

    def gather_y(t):
        return remote(rt.at[t, OWN], rt.at[t, PARTNER], y_s.at[t], y_r.at[t], index(0, PARTNER))

    def gather_c(t):
        return remote(rt.at[t, OWN], rt.at[t, SIBLING], c_s.at[t], c_r.at[t], index(0, SIBLING))

    def forward(t):
        return remote(rt.at[t, PARTNER], rt.at[t, DIAGONAL], f_s.at[t], f_r.at[t], index(0, SIBLING))

    def share(t, j):
        return remote(stat.at[t, OWN], stat.at[t, j], t_s.at[t, j], t_r.at[t, j], index(0, j))

    def sum_z(t, rz):
        return remote(send_z.at[t, rz], recv_z.at[t, m - rz], gz_s.at[t, rz], gz_r.at[t, m - rz], chunk(rz))

    def sum_c(t, i):
        return remote(send_c.at[t, i], recv_c.at[t, i], gc_s.at[t, i], gc_r.at[t, i], index(0, SIBLING))

    def sum_y(t):
        return remote(send_y.at[t], recv_y.at[t], gy_s.at[t], gy_r.at[t], index(0, PARTNER))

    barrier = pltpu.get_barrier_semaphore()
    for other in [chunk(g) for g in range(1, m)] + [index(0, j) for j in others]:
        pl.semaphore_signal(barrier, inc=1, device_id={"blk": other}, device_id_type=MESH)
    loads = [
        pltpu.make_async_copy(src, dst, in_s.at[i])
        for i, (src, dst) in enumerate(
            [(q_hbm, q_ref), (g_hbm, g_ref), (k_hbm, kv.at[KEY, 0]), (v_hbm, kv.at[VALUE, 0]),
             (mask_hbm, mask_ref), (order_hbm, order_ref)]
        )
    ]
    for load in loads:
        load.start()
    for t, ref in ((QUERY, q_ref), (GRAD, g_ref)):
        loads[t].wait()
        for h in range(heads):
            rt[t, OWN, :, h * tok:(h + 1) * tok] = ref[:, h * hd:(h + 1) * hd].T
    for load in loads[2:]:
        load.wait()
    pl.semaphore_wait(barrier, m + 2)

    far = sorted(range(1, m), key=lambda r: -min(r, m - r))
    for t in (0, 1):
        for rz in far:
            gather_z(t, rz).start()
        gather_y(t).start()
        gather_c(t).start()

    blocks = [order_ref[index(0, j)] for j in quad]
    key_ids = lax.broadcasted_iota(jnp.int32, (tok, rows), 0)
    row_ids = lax.broadcasted_iota(jnp.int32, (tok, rows), 1) % tok
    causal = jnp.where(row_ids >= key_ids, 0.0, MASKED).astype(F32)

    def bias(j, rz):
        if rz == 0 and j == OWN:
            return causal
        block = order_ref[chunk(rz)]
        seen = (blocks[j] > block) & (mask_ref[blocks[j], block] == 1)
        return jnp.where(seen, 0.0, MASKED).astype(F32)

    def flat(t):
        return kv[t].reshape(keys, hd)

    def score(j):
        scores = dot(flat(KEY), rt[QUERY, j])
        top = jnp.full((1, rows), 0.1 * MASKED, F32)
        parts = []
        for rz in range(m):
            s = scores[rz * tok:(rz + 1) * tok]
            b = bias(j, rz)
            if rz == 0 and j == OWN:
                s = s * to_exp2 + b
                top = jnp.maximum(top, jnp.max(s, axis=0, keepdims=True))
            else:
                top = jnp.maximum(top, jnp.max(s, axis=0, keepdims=True) * to_exp2 + b)
            parts.append((s, b))
        total = jnp.zeros((1, rows), F32)
        for rz, (s, b) in enumerate(parts):
            if rz == 0 and j == OWN:
                p = jnp.exp2(s - top)
            else:
                p = jnp.exp2(s * to_exp2 + (b - top))
            total = total + jnp.sum(p, axis=0, keepdims=True)
            prob[j, rz * tok:(rz + 1) * tok, :] = p.astype(BF16)
        mine[0, j] = top
        stat[0, OWN, :, j * rows:(j + 1) * rows] = top + jnp.log2(jnp.maximum(total, 1e-37))

    gather_y(QUERY).wait_recv()
    forward(QUERY).start()
    for rz in range(1, m):
        gather_z(KEY, rz).wait_recv()
    score(OWN)
    gather_c(QUERY).wait_recv()
    score(SIBLING)
    score(PARTNER)
    forward(QUERY).wait_recv()
    score(DIAGONAL)
    for j in others:
        share(0, j).start()

    def prob_grad(j):
        total = jnp.zeros((1, rows), F32)
        grads = dot(flat(VALUE), rt[GRAD, j])
        dprob[j] = grads
        mine[1, j] = jnp.sum(prob[j].astype(F32) * grads, axis=0, keepdims=True)

    gather_y(GRAD).wait_recv()
    forward(GRAD).start()
    for rz in range(1, m):
        gather_z(VALUE, rz).wait_recv()
    prob_grad(OWN)
    gather_c(GRAD).wait_recv()
    prob_grad(SIBLING)
    prob_grad(PARTNER)
    forward(GRAD).wait_recv()
    prob_grad(DIAGONAL)

    def shared(t, r, j):
        return stat[t, r, :, (r ^ j) * rows:((r ^ j) + 1) * rows]

    for j in others:
        share(0, j).wait_recv()
    factors = []
    for j in quad:
        parts = [shared(0, r, j) for r in quad]
        top = jnp.maximum(jnp.maximum(parts[0], parts[1]), jnp.maximum(parts[2], parts[3]))
        total = sum(jnp.exp2(part - top) for part in parts)
        factor = jnp.exp2(mine[0, j] - top - jnp.log2(total))
        factors.append(factor)
        stat[1, OWN, :, j * rows:(j + 1) * rows] = mine[1, j] * factor
    for j in others:
        share(1, j).start()

    def key_side(t):
        total = jnp.zeros((keys, hd), F32)
        for j in quad:
            scaled = (rt[t, j].astype(F32) * factors[j]).astype(BF16)
            total = total + dot_t(prob[j], scaled)
        return total

    def send_key_side(t, total):
        for rz in far:
            send_z[t, rz] = total[rz * tok:(rz + 1) * tok].astype(BF16)
            sum_z(t, rz).start()
        return total[:tok]

    def query_side(t, left, j, by):
        return dot(left, prob[j]) * (factors[j] * by)

    def start_query_side(t, left, by):
        send_c[t, 0] = query_side(t, left, DIAGONAL, by).astype(BF16)
        sum_c(t, 0).start()
        return query_side(t, left, PARTNER, by)

    def end_query_side(t, left, by, part):
        sum_c(t, 0).wait_recv()
        send_y[t] = (part + recv_c[t, 0].astype(F32)).astype(BF16)
        sum_y(t).start()
        send_c[t, 1] = query_side(t, left, SIBLING, by).astype(BF16)
        sum_c(t, 1).start()
        return query_side(t, left, OWN, by)

    def finish_query_side(t, total, out_ref):
        sum_c(t, 1).wait_recv()
        total = total + recv_c[t, 1].astype(F32)
        sum_y(t).wait_recv()
        total = (total + recv_y[t].astype(F32)).astype(BF16)
        for h in range(heads):
            out_ref[:, h * hd:(h + 1) * hd] = total[:, h * tok:(h + 1) * tok].T

    def finish_key_side(t, total, out_ref, by):
        for rz in reversed(far):
            sum_z(t, rz).wait_recv()
            total = total + recv_z[t, m - rz].astype(F32)
        out_ref[...] = total * by

    dv = send_key_side(VALUE, key_side(VALUE))
    values_t = flat(VALUE).T
    out_part = start_query_side(OUT, values_t, 1.0)
    out = end_query_side(OUT, values_t, 1.0, out_part)

    for j in others:
        share(1, j).wait_recv()
    for j in (DIAGONAL, PARTNER, SIBLING, OWN):
        delta = sum(shared(1, r, j) for r in quad)
        prob[j] = (prob[j].astype(F32) * (dprob[j] - delta)).astype(BF16)
    keys_t = flat(KEY).T
    dq_part = start_query_side(DQ, keys_t, scale)
    dk = send_key_side(KEY, key_side(KEY))
    dq = end_query_side(DQ, keys_t, scale, dq_part)

    finish_query_side(OUT, out, att_ref)
    finish_key_side(VALUE, dv, dv_ref, 1.0)
    finish_key_side(KEY, dk, dk_ref, scale)
    finish_query_side(DQ, dq, dq_ref)

    for t in (0, 1):
        gather_y(t).wait_send()
        gather_c(t).wait_send()
        forward(t).wait_send()
        sum_y(t).wait_send()
        for i in (0, 1):
            sum_c(t, i).wait_send()
        for j in others:
            share(t, j).wait_send()
        for rz in range(1, m):
            gather_z(t, rz).wait_send()
            sum_z(t, rz).wait_send()


def write_out(*refs):
    out_s = refs[8]
    stores = [pltpu.make_async_copy(refs[i], refs[4 + i], out_s.at[i]) for i in range(4)]
    for store in stores:
        store.start()
    for store in stores:
        store.wait()


def shards(queries, key_states, value_states, grad_out, tile_mask, block_order):
    n = lax.axis_size("blk")
    m = n // 4
    tok, hd = key_states.shape
    rows = queries.shape[1] // hd * tok
    assert n == 4 * m and tile_mask.shape[1] == n
    hbm = pl.BlockSpec(memory_space=pltpu.HBM)
    vmem = pl.BlockSpec(memory_space=pltpu.VMEM)
    dma = pltpu.SemaphoreType.DMA
    shapes = (
        jax.ShapeDtypeStruct(queries.shape, BF16),
        jax.ShapeDtypeStruct(queries.shape, BF16),
        jax.ShapeDtypeStruct(key_states.shape, F32),
        jax.ShapeDtypeStruct(key_states.shape, F32),
    )
    results = pl.pallas_call(
        functools.partial(kernel, n),
        out_shape=tuple(pltpu.VMEM(s.shape, s.dtype) for s in shapes),
        in_specs=[hbm] * 6,
        out_specs=(vmem,) * 4,
        scratch_shapes=[
            pltpu.SMEM(tile_mask.shape, jnp.int32),
            pltpu.SMEM(block_order.shape, jnp.int32),
            pltpu.VMEM(queries.shape, BF16),
            pltpu.VMEM(queries.shape, BF16),
            pltpu.VMEM((2, m, tok, hd), BF16),
            pltpu.VMEM((2, 4, hd, rows), BF16),
            pltpu.VMEM((4, m * tok, rows), BF16),
            pltpu.VMEM((4, m * tok, rows), F32),
            pltpu.VMEM((2, 4, 1, 4 * rows), F32),
            pltpu.VMEM((2, 4, 1, rows), F32),
            pltpu.VMEM((2, m, tok, hd), BF16),
            pltpu.VMEM((2, m, tok, hd), BF16),
            pltpu.VMEM((2, 2, hd, rows), BF16),
            pltpu.VMEM((2, 2, hd, rows), BF16),
            pltpu.VMEM((2, hd, rows), BF16),
            pltpu.VMEM((2, hd, rows), BF16),
            dma((6,)), dma((2, m)), dma((2, m)), dma((2,)), dma((2,)), dma((2,)), dma((2,)), dma((2,)), dma((2,)),
            dma((2, 4)), dma((2, 4)), dma((2, m)), dma((2, m)), dma((2, 2)), dma((2, 2)), dma((2,)), dma((2,)),
        ],
        compiler_params=pltpu.CompilerParams(
            collective_id=0, has_side_effects=True, vmem_limit_bytes=58 * 1024 * 1024
        ),
    )(queries, key_states, value_states, grad_out, tile_mask, block_order)
    return pl.pallas_call(
        write_out,
        out_shape=shapes,
        in_specs=[vmem] * 4,
        out_specs=(hbm,) * 4,
        scratch_shapes=[dma((4,))],
        compiler_params=pltpu.CompilerParams(vmem_limit_bytes=8 * 1024 * 1024),
    )(*results)


def solution(mesh):
    both = P(("groups", "blk"), None)
    return jax.shard_map(
        shards,
        mesh=mesh,
        in_specs=(both, both, both, both, P("groups", None), P("groups")),
        out_specs=(both, both, both, both),
        check_vma=False,
    )
```

```python
import functools
import math

import jax
import jax.numpy as jnp
from jax import lax
from jax.experimental import pallas as pl
from jax.experimental.pallas import tpu as pltpu
from jax.sharding import PartitionSpec as P

MESH = pl.DeviceIdType.MESH
F32 = jnp.float32
BF16 = jnp.bfloat16
MASKED = -1e30


def dot(a, b):
    return jnp.dot(a, b, preferred_element_type=F32)


def dot_t(a, b):
    return lax.dot_general(a, b, (((1,), (1,)), ((), ())), preferred_element_type=F32)


def kernel(
    n, q_hbm, k_hbm, v_hbm, g_hbm, mask_hbm, order_hbm, att_ref, dq_ref, dk_ref, dv_ref,
    mask_ref, order_ref, q_ref, g_ref, kv, rt, prob, prod, left, raw, stat, mine, send_z, recv_z, send_c, recv_c, send_y, recv_y,
    in_s, z_s, z_r, y_s, y_r, c_s, c_r, f_s, f_r, t_s, t_r, gz_s, gz_r, gc_s, gc_r, gy_s, gy_r,
):
    m = n // 4
    tok, hd = k_hbm.shape
    heads = q_hbm.shape[1] // hd
    rows = heads * tok
    keys = m * tok
    scale = hd ** -0.5
    to_exp2 = scale * math.log2(math.e)
    KEY, VALUE = 0, 1
    QUERY, GRAD = 0, 1
    OUT, DQ = 0, 1
    OWN, SIBLING, DIAGONAL, PARTNER = 0, 1, 2, 3
    quad = (OWN, SIBLING, DIAGONAL, PARTNER)
    others = (DIAGONAL, PARTNER, SIBLING)

    me = lax.axis_index("blk")
    z, y, c = me // 4, (me // 2) % 2, me % 2

    def index(rz, j):
        zz = lax.rem(z + rz, m)
        yy = 1 - y if j & 2 else y
        cc = 1 - c if j & 1 else c
        return (zz * 2 + yy) * 2 + cc

    def chunk(rz):
        return index(rz, 1 if rz else 0)

    def remote(src, dst, s_sem, r_sem, target):
        return pltpu.make_async_remote_copy(
            src_ref=src, dst_ref=dst, send_sem=s_sem, recv_sem=r_sem,
            device_id={"blk": target}, device_id_type=MESH,
        )

    def gather_z(t, g):
        return remote(kv.at[t, 0], kv.at[t, m - g], z_s.at[t, g], z_r.at[t, m - g], chunk(g))

    def gather_y(t):
        return remote(rt.at[t, OWN], rt.at[t, PARTNER], y_s.at[t], y_r.at[t], index(0, PARTNER))

    def gather_c(t):
        return remote(rt.at[t, OWN], rt.at[t, SIBLING], c_s.at[t], c_r.at[t], index(0, SIBLING))

    def forward(t):
        return remote(rt.at[t, PARTNER], rt.at[t, DIAGONAL], f_s.at[t], f_r.at[t], index(0, SIBLING))

    def share(t, j):
        return remote(stat.at[t, OWN], stat.at[t, j], t_s.at[t, j], t_r.at[t, j], index(0, j))

    def sum_z(t, rz):
        return remote(send_z.at[t, rz], recv_z.at[t, m - rz], gz_s.at[t, rz], gz_r.at[t, m - rz], chunk(rz))

    def sum_c(t, i):
        return remote(send_c.at[t, i], recv_c.at[t, i], gc_s.at[t, i], gc_r.at[t, i], index(0, SIBLING))

    def sum_y(t):
        return remote(send_y.at[t], recv_y.at[t], gy_s.at[t], gy_r.at[t], index(0, PARTNER))

    barrier = pltpu.get_barrier_semaphore()
    for other in [chunk(g) for g in range(1, m)] + [index(0, j) for j in others]:
        pl.semaphore_signal(barrier, inc=1, device_id={"blk": other}, device_id_type=MESH)
    loads = [
        pltpu.make_async_copy(src, dst, in_s.at[i])
        for i, (src, dst) in enumerate(
            [(q_hbm, q_ref), (g_hbm, g_ref), (k_hbm, kv.at[KEY, 0]), (v_hbm, kv.at[VALUE, 0]),
             (mask_hbm, mask_ref), (order_hbm, order_ref)]
        )
    ]
    for load in loads:
        load.start()
    for t, ref in ((QUERY, q_ref), (GRAD, g_ref)):
        loads[t].wait()
        for h in range(heads):
            rt[t, OWN, :, h * tok:(h + 1) * tok] = ref[:, h * hd:(h + 1) * hd].T
    for load in loads[2:]:
        load.wait()
    pl.semaphore_wait(barrier, m + 2)

    far = sorted(range(1, m), key=lambda r: -min(r, m - r))
    for t in (0, 1):
        for rz in far:
            gather_z(t, rz).start()
        gather_y(t).start()
        gather_c(t).start()

    blocks = [order_ref[index(0, j)] for j in quad]
    key_ids = lax.broadcasted_iota(jnp.int32, (tok, rows), 0)
    row_ids = lax.broadcasted_iota(jnp.int32, (tok, rows), 1) % tok
    causal = jnp.where(row_ids >= key_ids, 0.0, MASKED).astype(F32)

    def bias(j, rz):
        if rz == 0 and j == OWN:
            return causal
        block = order_ref[chunk(rz)]
        seen = (blocks[j] > block) & (mask_ref[blocks[j], block] == 1)
        return jnp.where(seen, 0.0, MASKED).astype(F32)

    def flat(t):
        return kv[t].reshape(keys, hd)

    def score(j):
        scores = dot(flat(KEY), rt[QUERY, j])
        top = jnp.full((1, rows), 0.1 * MASKED, F32)
        parts = []
        for rz in range(m):
            s = scores[rz * tok:(rz + 1) * tok]
            b = bias(j, rz)
            if rz == 0 and j == OWN:
                s = s * to_exp2 + b
                top = jnp.maximum(top, jnp.max(s, axis=0, keepdims=True))
            else:
                top = jnp.maximum(top, jnp.max(s, axis=0, keepdims=True) * to_exp2 + b)
            parts.append((s, b))
        total = jnp.zeros((1, rows), F32)
        for rz, (s, b) in enumerate(parts):
            if rz == 0 and j == OWN:
                p = jnp.exp2(s - top)
            else:
                p = jnp.exp2(s * to_exp2 + (b - top))
            total = total + jnp.sum(p, axis=0, keepdims=True)
            prob[j, rz * tok:(rz + 1) * tok, :] = p.astype(BF16)
        mine[0, j] = top
        stat[0, OWN, :, j * rows:(j + 1) * rows] = top + jnp.log2(jnp.maximum(total, 1e-37))

    gather_y(QUERY).wait_recv()
    forward(QUERY).start()
    for rz in range(1, m):
        gather_z(KEY, rz).wait_recv()
    score(OWN)
    gather_c(QUERY).wait_recv()
    score(SIBLING)
    score(PARTNER)
    forward(QUERY).wait_recv()
    score(DIAGONAL)
    for j in others:
        share(0, j).start()

    def prob_grad(j):
        grads = dot(flat(VALUE), rt[GRAD, j])
        grads = prob[j].astype(F32) * grads
        mine[1, j] = jnp.sum(grads, axis=0, keepdims=True)
        prod[j] = grads.astype(BF16)
        raw[j, :2 * hd] = dot(left[...], prob[j])
        raw[j, 2 * hd:] = dot(left[hd:], prod[j])

    gather_y(GRAD).wait_recv()
    forward(GRAD).start()
    for rz in range(1, m):
        gather_z(VALUE, rz).wait_recv()
    left[:hd] = flat(VALUE).T
    left[hd:] = flat(KEY).T
    prob_grad(OWN)
    gather_c(GRAD).wait_recv()
    prob_grad(SIBLING)
    prob_grad(PARTNER)
    forward(GRAD).wait_recv()
    prob_grad(DIAGONAL)

    def shared(t, r, j):
        return stat[t, r, :, (r ^ j) * rows:((r ^ j) + 1) * rows]

    for j in others:
        share(0, j).wait_recv()
    factors = []
    for j in quad:
        parts = [shared(0, r, j) for r in quad]
        top = jnp.maximum(jnp.maximum(parts[0], parts[1]), jnp.maximum(parts[2], parts[3]))
        total = sum(jnp.exp2(part - top) for part in parts)
        factor = jnp.exp2(mine[0, j] - top - jnp.log2(total))
        factors.append(factor)
        stat[1, OWN, :, j * rows:(j + 1) * rows] = mine[1, j] * factor
    for j in others:
        share(1, j).start()

    def key_side(weights, sides):
        total = jnp.zeros((keys, hd), F32)
        for j in quad:
            total = total + dot_t(weights[j], sides[j])
        return total

    def send_key_side(t, total):
        for rz in far:
            send_z[t, rz] = total[rz * tok:(rz + 1) * tok].astype(BF16)
            sum_z(t, rz).start()
        return total[:tok]

    def start_query_side(t, part):
        send_c[t, 0] = part(DIAGONAL).astype(BF16)
        sum_c(t, 0).start()

    def pass_query_side(t, part):
        total = part(PARTNER)
        sum_c(t, 0).wait_recv()
        send_y[t] = (total + recv_c[t, 0].astype(F32)).astype(BF16)
        sum_y(t).start()
        send_c[t, 1] = part(SIBLING).astype(BF16)
        sum_c(t, 1).start()

    def out_part(j):
        return raw[j, :hd] * factors[j]

    def dq_part(j):
        return (raw[j, 2 * hd:] - raw[j, hd:2 * hd] * deltas[j]) * (factors[j] * scale)

    def finish_query_side(t, total, out_ref):
        sum_c(t, 1).wait_recv()
        total = total + recv_c[t, 1].astype(F32)
        sum_y(t).wait_recv()
        total = (total + recv_y[t].astype(F32)).astype(BF16)
        for h in range(heads):
            out_ref[:, h * hd:(h + 1) * hd] = total[:, h * tok:(h + 1) * tok].T

    def finish_key_side(t, total, out_ref, by):
        for rz in reversed(far):
            sum_z(t, rz).wait_recv()
            total = total + recv_z[t, m - rz].astype(F32)
        out_ref[...] = total * by

    start_query_side(OUT, out_part)
    scaled = [(rt[GRAD, j].astype(F32) * factors[j]).astype(BF16) for j in quad]
    dv = send_key_side(VALUE, key_side(prob, scaled))
    pass_query_side(OUT, out_part)
    scaled = [rt[QUERY, j].astype(F32) * factors[j] for j in quad]
    first = key_side(prod, [side.astype(BF16) for side in scaled])

    for j in others:
        share(1, j).wait_recv()
    deltas = [sum(shared(1, r, j) for r in quad) for j in quad]
    start_query_side(DQ, dq_part)
    dk = first - key_side(prob, [(side * delta).astype(BF16) for side, delta in zip(scaled, deltas)])
    dk = send_key_side(KEY, dk)
    pass_query_side(DQ, dq_part)

    finish_query_side(OUT, out_part(OWN), att_ref)
    finish_key_side(VALUE, dv, dv_ref, 1.0)
    finish_key_side(KEY, dk, dk_ref, scale)
    finish_query_side(DQ, dq_part(OWN), dq_ref)

    for t in (0, 1):
        gather_y(t).wait_send()
        gather_c(t).wait_send()
        forward(t).wait_send()
        sum_y(t).wait_send()
        for i in (0, 1):
            sum_c(t, i).wait_send()
        for j in others:
            share(t, j).wait_send()
        for rz in range(1, m):
            gather_z(t, rz).wait_send()
            sum_z(t, rz).wait_send()


def write_out(*refs):
    out_s = refs[8]
    stores = [pltpu.make_async_copy(refs[i], refs[4 + i], out_s.at[i]) for i in range(4)]
    for store in stores:
        store.start()
    for store in stores:
        store.wait()


def shards(queries, key_states, value_states, grad_out, tile_mask, block_order):
    n = lax.axis_size("blk")
    m = n // 4
    tok, hd = key_states.shape
    rows = queries.shape[1] // hd * tok
    assert n == 4 * m and tile_mask.shape[1] == n
    hbm = pl.BlockSpec(memory_space=pltpu.HBM)
    vmem = pl.BlockSpec(memory_space=pltpu.VMEM)
    dma = pltpu.SemaphoreType.DMA
    shapes = (
        jax.ShapeDtypeStruct(queries.shape, BF16),
        jax.ShapeDtypeStruct(queries.shape, BF16),
        jax.ShapeDtypeStruct(key_states.shape, F32),
        jax.ShapeDtypeStruct(key_states.shape, F32),
    )
    results = pl.pallas_call(
        functools.partial(kernel, n),
        out_shape=tuple(pltpu.VMEM(s.shape, s.dtype) for s in shapes),
        in_specs=[hbm] * 6,
        out_specs=(vmem,) * 4,
        scratch_shapes=[
            pltpu.SMEM(tile_mask.shape, jnp.int32),
            pltpu.SMEM(block_order.shape, jnp.int32),
            pltpu.VMEM(queries.shape, BF16),
            pltpu.VMEM(queries.shape, BF16),
            pltpu.VMEM((2, m, tok, hd), BF16),
            pltpu.VMEM((2, 4, hd, rows), BF16),
            pltpu.VMEM((4, m * tok, rows), BF16),
            pltpu.VMEM((4, m * tok, rows), BF16),
            pltpu.VMEM((2 * hd, m * tok), BF16),
            pltpu.VMEM((4, 3 * hd, rows), F32),
            pltpu.VMEM((2, 4, 1, 4 * rows), F32),
            pltpu.VMEM((2, 4, 1, rows), F32),
            pltpu.VMEM((2, m, tok, hd), BF16),
            pltpu.VMEM((2, m, tok, hd), BF16),
            pltpu.VMEM((2, 2, hd, rows), BF16),
            pltpu.VMEM((2, 2, hd, rows), BF16),
            pltpu.VMEM((2, hd, rows), BF16),
            pltpu.VMEM((2, hd, rows), BF16),
            dma((6,)), dma((2, m)), dma((2, m)), dma((2,)), dma((2,)), dma((2,)), dma((2,)), dma((2,)), dma((2,)),
            dma((2, 4)), dma((2, 4)), dma((2, m)), dma((2, m)), dma((2, 2)), dma((2, 2)), dma((2,)), dma((2,)),
        ],
        compiler_params=pltpu.CompilerParams(
            collective_id=0, has_side_effects=True, vmem_limit_bytes=58 * 1024 * 1024
        ),
    )(queries, key_states, value_states, grad_out, tile_mask, block_order)
    return pl.pallas_call(
        write_out,
        out_shape=shapes,
        in_specs=[vmem] * 4,
        out_specs=(hbm,) * 4,
        scratch_shapes=[dma((4,))],
        compiler_params=pltpu.CompilerParams(vmem_limit_bytes=8 * 1024 * 1024),
    )(*results)


def solution(mesh):
    both = P(("groups", "blk"), None)
    return jax.shard_map(
        shards,
        mesh=mesh,
        in_specs=(both, both, both, both, P("groups", None), P("groups")),
        out_specs=(both, both, both, both),
        check_vma=False,
    )
```

```python
import functools
import math

import jax
import jax.numpy as jnp
from jax import lax
from jax.experimental import pallas as pl
from jax.experimental.pallas import tpu as pltpu
from jax.sharding import PartitionSpec as P

MESH = pl.DeviceIdType.MESH
F32 = jnp.float32
BF16 = jnp.bfloat16
MASKED = -1e30


def dot(a, b):
    return jnp.dot(a, b, preferred_element_type=F32)


def dot_t(a, b):
    return lax.dot_general(a, b, (((1,), (1,)), ((), ())), preferred_element_type=F32)


def kernel(
    n, q_hbm, k_hbm, v_hbm, g_hbm, mask_hbm, order_hbm, att_ref, dq_ref, dk_ref, dv_ref,
    mask_ref, order_ref, q_ref, g_ref, kv, rt, prob, prod, left, raw, stat, mine, send_z, recv_z, send_c, recv_c, send_y, recv_y,
    in_s, z_s, z_r, y_s, y_r, c_s, c_r, f_s, f_r, t_s, t_r, gz_s, gz_r, gc_s, gc_r, gy_s, gy_r,
):
    m = n // 4
    tok, hd = k_hbm.shape
    heads = q_hbm.shape[1] // hd
    rows = heads * tok
    keys = m * tok
    scale = hd ** -0.5
    to_exp2 = scale * math.log2(math.e)
    KEY, VALUE = 0, 1
    QUERY, GRAD = 0, 1
    OUT, DQ = 0, 1
    OWN, SIBLING, DIAGONAL, PARTNER = 0, 1, 2, 3
    quad = (OWN, SIBLING, DIAGONAL, PARTNER)
    others = (DIAGONAL, PARTNER, SIBLING)

    me = lax.axis_index("blk")
    z, y, c = me // 4, (me // 2) % 2, me % 2

    def index(rz, j):
        zz = lax.rem(z + rz, m)
        yy = 1 - y if j & 2 else y
        cc = 1 - c if j & 1 else c
        return (zz * 2 + yy) * 2 + cc

    def chunk(rz):
        return index(rz, 1 if rz else 0)

    def remote(src, dst, s_sem, r_sem, target):
        return pltpu.make_async_remote_copy(
            src_ref=src, dst_ref=dst, send_sem=s_sem, recv_sem=r_sem,
            device_id={"blk": target}, device_id_type=MESH,
        )

    def gather_z(t, g):
        return remote(kv.at[t, 0], kv.at[t, m - g], z_s.at[t, g], z_r.at[t, m - g], chunk(g))

    def gather_y(t):
        return remote(rt.at[t, OWN], rt.at[t, PARTNER], y_s.at[t], y_r.at[t], index(0, PARTNER))

    def gather_c(t):
        return remote(rt.at[t, OWN], rt.at[t, SIBLING], c_s.at[t], c_r.at[t], index(0, SIBLING))

    def forward(t):
        return remote(rt.at[t, PARTNER], rt.at[t, DIAGONAL], f_s.at[t], f_r.at[t], index(0, SIBLING))

    def share(t, j):
        return remote(stat.at[t, OWN], stat.at[t, j], t_s.at[t, j], t_r.at[t, j], index(0, j))

    def sum_z(t, rz):
        return remote(send_z.at[t, rz], recv_z.at[t, m - rz], gz_s.at[t, rz], gz_r.at[t, m - rz], chunk(rz))

    def sum_c(t, i):
        part = pl.ds(2 * hd, hd) if t else pl.ds(0, 2 * hd)
        return remote(send_c.at[i, part], recv_c.at[i, part], gc_s.at[t, i], gc_r.at[t, i], index(0, SIBLING))

    def sum_y(t):
        return remote(send_y.at[t], recv_y.at[t], gy_s.at[t], gy_r.at[t], index(0, PARTNER))

    barrier = pltpu.get_barrier_semaphore()
    for other in [chunk(g) for g in range(1, m)] + [index(0, j) for j in others]:
        pl.semaphore_signal(barrier, inc=1, device_id={"blk": other}, device_id_type=MESH)
    loads = [
        pltpu.make_async_copy(src, dst, in_s.at[i])
        for i, (src, dst) in enumerate(
            [(q_hbm, q_ref), (g_hbm, g_ref), (k_hbm, kv.at[KEY, 0]), (v_hbm, kv.at[VALUE, 0]),
             (mask_hbm, mask_ref), (order_hbm, order_ref)]
        )
    ]
    for load in loads:
        load.start()
    for t, ref in ((QUERY, q_ref), (GRAD, g_ref)):
        loads[t].wait()
        for h in range(heads):
            rt[t, OWN, :, h * tok:(h + 1) * tok] = ref[:, h * hd:(h + 1) * hd].T
    for load in loads[2:]:
        load.wait()
    pl.semaphore_wait(barrier, m + 2)

    far = sorted(range(1, m), key=lambda r: -min(r, m - r))
    for t in (0, 1):
        gather_y(t).start()
        for rz in far:
            gather_z(t, rz).start()
        gather_c(t).start()

    blocks = [order_ref[index(0, j)] for j in quad]
    key_ids = lax.broadcasted_iota(jnp.int32, (tok, rows), 0)
    row_ids = lax.broadcasted_iota(jnp.int32, (tok, rows), 1) % tok
    causal = jnp.where(row_ids >= key_ids, 0.0, MASKED).astype(F32)

    def bias(j, rz):
        if rz == 0 and j == OWN:
            return causal
        block = order_ref[chunk(rz)]
        seen = (blocks[j] > block) & (mask_ref[blocks[j], block] == 1)
        return jnp.where(seen, 0.0, MASKED).astype(F32)

    def flat(t):
        return kv[t].reshape(keys, hd)

    def score(j):
        scores = dot(flat(KEY), rt[QUERY, j])
        top = jnp.full((1, rows), 0.1 * MASKED, F32)
        parts = []
        for rz in range(m):
            s = scores[rz * tok:(rz + 1) * tok]
            b = bias(j, rz)
            if rz == 0 and j == OWN:
                s = s * to_exp2 + b
                top = jnp.maximum(top, jnp.max(s, axis=0, keepdims=True))
            else:
                top = jnp.maximum(top, jnp.max(s, axis=0, keepdims=True) * to_exp2 + b)
            parts.append((s, b))
        total = jnp.zeros((1, rows), F32)
        for rz, (s, b) in enumerate(parts):
            if rz == 0 and j == OWN:
                p = jnp.exp2(s - top)
            else:
                p = jnp.exp2(s * to_exp2 + (b - top))
            total = total + jnp.sum(p, axis=0, keepdims=True)
            prob[j, rz * tok:(rz + 1) * tok, :] = p.astype(BF16)
        log_sum = top + jnp.log2(jnp.maximum(total, 1e-37))
        mine[0, j] = top
        mine[1, j] = jnp.exp2(top - log_sum)
        stat[0, OWN, :, j * rows:(j + 1) * rows] = log_sum

    gather_y(QUERY).wait_recv()
    forward(QUERY).start()
    for rz in range(1, m):
        gather_z(KEY, rz).wait_recv()
    score(OWN)
    gather_c(QUERY).wait_recv()
    score(SIBLING)
    score(PARTNER)
    forward(QUERY).wait_recv()
    score(DIAGONAL)
    for j in others:
        share(0, j).start()

    def query_side(j, t):
        part = slice(2 * hd, 3 * hd) if t else slice(0, 2 * hd)
        product = dot(left[hd:], prod[j]) if t else dot(left[...], prob[j])
        if j & 1 == j >> 1:
            raw[0 if j else 1, part] = product
        else:
            i = 0 if j == DIAGONAL else 1
            send_c[i, part] = (product * mine[1, j]).astype(BF16)
            sum_c(t, i).start()

    def prob_grad(j):
        grads = prob[j].astype(F32) * dot(flat(VALUE), rt[GRAD, j])
        prod[j] = grads.astype(BF16)
        stat[1, OWN, :, j * rows:(j + 1) * rows] = jnp.sum(grads, axis=0, keepdims=True) * mine[1, j]

    gather_y(GRAD).wait_recv()
    forward(GRAD).start()
    for rz in range(1, m):
        gather_z(VALUE, rz).wait_recv()
    left[:hd] = flat(VALUE).T
    left[hd:] = flat(KEY).T
    for j in (DIAGONAL, SIBLING, PARTNER, OWN):
        query_side(j, 0)
    prob_grad(OWN)
    gather_c(GRAD).wait_recv()
    prob_grad(SIBLING)
    prob_grad(PARTNER)
    forward(GRAD).wait_recv()
    prob_grad(DIAGONAL)
    for j in others:
        share(1, j).start()
    for j in (DIAGONAL, SIBLING, PARTNER, OWN):
        query_side(j, 1)

    def shared(t, r, j):
        return stat[t, r, :, (r ^ j) * rows:((r ^ j) + 1) * rows]

    for j in others:
        share(0, j).wait_recv()
    shares, factors = [], []
    for j in quad:
        parts = [shared(0, r, j) for r in quad]
        top = jnp.maximum(jnp.maximum(parts[0], parts[1]), jnp.maximum(parts[2], parts[3]))
        log_sum = top + jnp.log2(sum(jnp.exp2(part - top) for part in parts))
        shares.append([jnp.exp2(part - log_sum) for part in parts])
        factors.append(jnp.exp2(mine[0, j] - log_sum))

    def key_side(weights, sides):
        total = jnp.zeros((keys, hd), F32)
        for j in quad:
            total = total + dot_t(weights[j], sides[j])
        return total

    def send_key_side(t, total):
        for rz in far:
            send_z[t, rz] = total[rz * tok:(rz + 1) * tok].astype(BF16)
            sum_z(t, rz).start()
        return total[:tok]

    def both_cores(i, t):
        j = OWN if i else PARTNER
        part = slice(t * hd, (t + 1) * hd)
        return raw[i, part] * factors[j] + recv_c[i, part].astype(F32) * shares[j][SIBLING]

    def out_part(i):
        return both_cores(i, 0)

    def dq_part(i):
        return (both_cores(i, 2) - both_cores(i, 1) * deltas[OWN if i else PARTNER]) * scale

    def pass_query_side(t, part):
        sum_c(t, 0).wait_recv()
        send_y[t] = part(0).astype(BF16)
        sum_y(t).start()

    def finish_query_side(t, total, out_ref):
        sum_y(t).wait_recv()
        total = (total + recv_y[t].astype(F32)).astype(BF16)
        for h in range(heads):
            out_ref[:, h * hd:(h + 1) * hd] = total[:, h * tok:(h + 1) * tok].T

    def finish_key_side(t, total, out_ref, by):
        for rz in reversed(far):
            sum_z(t, rz).wait_recv()
            total = total + recv_z[t, m - rz].astype(F32)
        out_ref[...] = total * by

    pass_query_side(OUT, out_part)
    scaled = [(rt[GRAD, j].astype(F32) * factors[j]).astype(BF16) for j in quad]
    dv = send_key_side(VALUE, key_side(prob, scaled))
    scaled = [rt[QUERY, j].astype(F32) * factors[j] for j in quad]
    first = key_side(prod, [side.astype(BF16) for side in scaled])

    for j in others:
        share(1, j).wait_recv()
    deltas = [sum(shared(1, r, j) * shares[j][r] for r in quad) for j in quad]
    pass_query_side(DQ, dq_part)
    dk = first - key_side(prob, [(side * delta).astype(BF16) for side, delta in zip(scaled, deltas)])
    dk = send_key_side(KEY, dk)

    sum_c(OUT, 1).wait_recv()
    finish_query_side(OUT, out_part(1), att_ref)
    finish_key_side(VALUE, dv, dv_ref, 1.0)
    finish_key_side(KEY, dk, dk_ref, scale)
    sum_c(DQ, 1).wait_recv()
    finish_query_side(DQ, dq_part(1), dq_ref)

    for t in (0, 1):
        gather_y(t).wait_send()
        gather_c(t).wait_send()
        forward(t).wait_send()
        sum_y(t).wait_send()
        for i in (0, 1):
            sum_c(t, i).wait_send()
        for j in others:
            share(t, j).wait_send()
        for rz in range(1, m):
            gather_z(t, rz).wait_send()
            sum_z(t, rz).wait_send()


def write_out(*refs):
    out_s = refs[8]
    stores = [pltpu.make_async_copy(refs[i], refs[4 + i], out_s.at[i]) for i in range(4)]
    for store in stores:
        store.start()
    for store in stores:
        store.wait()


def shards(queries, key_states, value_states, grad_out, tile_mask, block_order):
    n = lax.axis_size("blk")
    m = n // 4
    tok, hd = key_states.shape
    rows = queries.shape[1] // hd * tok
    assert n == 4 * m and tile_mask.shape[1] == n
    hbm = pl.BlockSpec(memory_space=pltpu.HBM)
    vmem = pl.BlockSpec(memory_space=pltpu.VMEM)
    dma = pltpu.SemaphoreType.DMA
    shapes = (
        jax.ShapeDtypeStruct(queries.shape, BF16),
        jax.ShapeDtypeStruct(queries.shape, BF16),
        jax.ShapeDtypeStruct(key_states.shape, F32),
        jax.ShapeDtypeStruct(key_states.shape, F32),
    )
    results = pl.pallas_call(
        functools.partial(kernel, n),
        out_shape=tuple(pltpu.VMEM(s.shape, s.dtype) for s in shapes),
        in_specs=[hbm] * 6,
        out_specs=(vmem,) * 4,
        scratch_shapes=[
            pltpu.SMEM(tile_mask.shape, jnp.int32),
            pltpu.SMEM(block_order.shape, jnp.int32),
            pltpu.VMEM(queries.shape, BF16),
            pltpu.VMEM(queries.shape, BF16),
            pltpu.VMEM((2, m, tok, hd), BF16),
            pltpu.VMEM((2, 4, hd, rows), BF16),
            pltpu.VMEM((4, m * tok, rows), BF16),
            pltpu.VMEM((4, m * tok, rows), BF16),
            pltpu.VMEM((2 * hd, m * tok), BF16),
            pltpu.VMEM((2, 3 * hd, rows), F32),
            pltpu.VMEM((2, 4, 1, 4 * rows), F32),
            pltpu.VMEM((2, 4, 1, rows), F32),
            pltpu.VMEM((2, m, tok, hd), BF16),
            pltpu.VMEM((2, m, tok, hd), BF16),
            pltpu.VMEM((2, 3 * hd, rows), BF16),
            pltpu.VMEM((2, 3 * hd, rows), BF16),
            pltpu.VMEM((2, hd, rows), BF16),
            pltpu.VMEM((2, hd, rows), BF16),
            dma((6,)), dma((2, m)), dma((2, m)), dma((2,)), dma((2,)), dma((2,)), dma((2,)), dma((2,)), dma((2,)),
            dma((2, 4)), dma((2, 4)), dma((2, m)), dma((2, m)), dma((2, 2)), dma((2, 2)), dma((2,)), dma((2,)),
        ],
        compiler_params=pltpu.CompilerParams(
            collective_id=0, has_side_effects=True, vmem_limit_bytes=58 * 1024 * 1024
        ),
    )(queries, key_states, value_states, grad_out, tile_mask, block_order)
    return pl.pallas_call(
        write_out,
        out_shape=shapes,
        in_specs=[vmem] * 4,
        out_specs=(hbm,) * 4,
        scratch_shapes=[dma((4,))],
        compiler_params=pltpu.CompilerParams(vmem_limit_bytes=8 * 1024 * 1024),
    )(*results)


def solution(mesh):
    both = P(("groups", "blk"), None)
    return jax.shard_map(
        shards,
        mesh=mesh,
        in_specs=(both, both, both, both, P("groups", None), P("groups")),
        out_specs=(both, both, both, both),
        check_vma=False,
    )
```

```python
import functools
import math

import jax
import jax.numpy as jnp
from jax import lax
from jax.experimental import pallas as pl
from jax.experimental.pallas import tpu as pltpu
from jax.sharding import PartitionSpec as P

MESH = pl.DeviceIdType.MESH
F32 = jnp.float32
BF16 = jnp.bfloat16
MASKED = -1e30


def dot(a, b):
    return jnp.dot(a, b, preferred_element_type=F32)


def dot_t(a, b):
    return lax.dot_general(a, b, (((1,), (1,)), ((), ())), preferred_element_type=F32)


def kernel(
    n, q_hbm, k_hbm, v_hbm, g_hbm, mask_hbm, order_hbm, att_ref, dq_ref, dk_ref, dv_ref,
    mask_ref, order_ref, q_ref, g_ref, kv, rt, prob, prod, left, raw, stat, mine, send_z, recv_z, send_c, recv_c, send_y, recv_y,
    in_s, z_s, z_r, y_s, y_r, c_s, c_r, f_s, f_r, t_s, t_r, gz_s, gz_r, gc_s, gc_r, gy_s, gy_r,
):
    m = n // 4
    tok, hd = k_hbm.shape
    heads = q_hbm.shape[1] // hd
    rows = heads * tok
    keys = m * tok
    scale = hd ** -0.5
    to_exp2 = scale * math.log2(math.e)
    KEY, VALUE = 0, 1
    QUERY, GRAD = 0, 1
    OUT, DQ = 0, 1
    OWN, SIBLING, DIAGONAL, PARTNER = 0, 1, 2, 3
    quad = (OWN, SIBLING, DIAGONAL, PARTNER)
    others = (DIAGONAL, PARTNER, SIBLING)

    me = lax.axis_index("blk")
    z, y, c = me // 4, (me // 2) % 2, me % 2

    def index(rz, j):
        zz = lax.rem(z + rz, m)
        yy = 1 - y if j & 2 else y
        cc = 1 - c if j & 1 else c
        return (zz * 2 + yy) * 2 + cc

    def chunk(rz):
        return index(rz, 1 if rz else 0)

    def remote(src, dst, s_sem, r_sem, target):
        return pltpu.make_async_remote_copy(
            src_ref=src, dst_ref=dst, send_sem=s_sem, recv_sem=r_sem,
            device_id={"blk": target}, device_id_type=MESH,
        )

    def gather_z(t, g):
        return remote(kv.at[t, 0], kv.at[t, m - g], z_s.at[t, g], z_r.at[t, m - g], chunk(g))

    def gather_y(t):
        return remote(rt.at[t, OWN], rt.at[t, PARTNER], y_s.at[t], y_r.at[t], index(0, PARTNER))

    def gather_c():
        return remote(rt.at[:, OWN], rt.at[:, SIBLING], c_s.at[0], c_r.at[0], index(0, SIBLING))

    def forward(t):
        return remote(rt.at[t, PARTNER], rt.at[t, DIAGONAL], f_s.at[t], f_r.at[t], index(0, SIBLING))

    def share(t, j):
        return remote(stat.at[t, OWN], stat.at[t, j], t_s.at[t, j], t_r.at[t, j], index(0, j))

    def sum_z(t, rz):
        return remote(send_z.at[t, rz], recv_z.at[t, m - rz], gz_s.at[t, rz], gz_r.at[t, m - rz], chunk(rz))

    def sum_c(t, i):
        part = pl.ds(2 * hd, hd) if t else pl.ds(0, 2 * hd)
        return remote(send_c.at[i, part], recv_c.at[i, part], gc_s.at[t, i], gc_r.at[t, i], index(0, SIBLING))

    def sum_y(t):
        return remote(send_y.at[t], recv_y.at[t], gy_s.at[t], gy_r.at[t], index(0, PARTNER))

    barrier = pltpu.get_barrier_semaphore()
    for other in [chunk(g) for g in range(1, m)] + [index(0, j) for j in others]:
        pl.semaphore_signal(barrier, inc=1, device_id={"blk": other}, device_id_type=MESH)
    loads = [
        pltpu.make_async_copy(src, dst, in_s.at[i])
        for i, (src, dst) in enumerate(
            [(q_hbm, q_ref), (g_hbm, g_ref), (k_hbm, kv.at[KEY, 0]), (v_hbm, kv.at[VALUE, 0]),
             (mask_hbm, mask_ref), (order_hbm, order_ref)]
        )
    ]
    for load in loads:
        load.start()
    for t, ref in ((QUERY, q_ref), (GRAD, g_ref)):
        loads[t].wait()
        for h in range(heads):
            rt[t, OWN, :, h * tok:(h + 1) * tok] = ref[:, h * hd:(h + 1) * hd].T
    for load in loads[2:]:
        load.wait()
    pl.semaphore_wait(barrier, m + 2)

    far = sorted(range(1, m), key=lambda r: -min(r, m - r))
    for t in (0, 1):
        gather_y(t).start()
        for rz in far:
            gather_z(t, rz).start()
        if t == 0:
            gather_c().start()

    blocks = [order_ref[index(0, j)] for j in quad]
    key_ids = lax.broadcasted_iota(jnp.int32, (tok, rows), 0)
    row_ids = lax.broadcasted_iota(jnp.int32, (tok, rows), 1) % tok
    causal = jnp.where(row_ids >= key_ids, 0.0, MASKED).astype(F32)

    def bias(j, rz):
        if rz == 0 and j == OWN:
            return causal
        block = order_ref[chunk(rz)]
        seen = (blocks[j] > block) & (mask_ref[blocks[j], block] == 1)
        return jnp.where(seen, 0.0, MASKED).astype(F32)

    def flat(t):
        return kv[t].reshape(keys, hd)

    def score(j):
        scores = dot(flat(KEY), rt[QUERY, j])
        top = jnp.full((1, rows), 0.1 * MASKED, F32)
        parts = []
        for rz in range(m):
            s = scores[rz * tok:(rz + 1) * tok]
            b = bias(j, rz)
            if rz == 0 and j == OWN:
                s = s * to_exp2 + b
                top = jnp.maximum(top, jnp.max(s, axis=0, keepdims=True))
            else:
                top = jnp.maximum(top, jnp.max(s, axis=0, keepdims=True) * to_exp2 + b)
            parts.append((s, b))
        total = jnp.zeros((1, rows), F32)
        for rz, (s, b) in enumerate(parts):
            if rz == 0 and j == OWN:
                p = jnp.exp2(s - top)
            else:
                p = jnp.exp2(s * to_exp2 + (b - top))
            total = total + jnp.sum(p, axis=0, keepdims=True)
            prob[j, rz * tok:(rz + 1) * tok, :] = p.astype(BF16)
        log_sum = top + jnp.log2(jnp.maximum(total, 1e-37))
        mine[0, j] = top
        mine[1, j] = jnp.exp2(top - log_sum)
        stat[0, OWN, :, j * rows:(j + 1) * rows] = log_sum

    gather_y(QUERY).wait_recv()
    forward(QUERY).start()
    for rz in range(1, m):
        gather_z(KEY, rz).wait_recv()
    score(OWN)
    gather_c().wait_recv()
    score(SIBLING)
    score(PARTNER)
    forward(QUERY).wait_recv()
    score(DIAGONAL)
    for j in others:
        share(0, j).start()
    left[hd:] = flat(KEY).T

    def query_side(j, t):
        part = slice(2 * hd, 3 * hd) if t else slice(0, 2 * hd)
        product = dot(left[hd:], prod[j]) if t else dot(left[...], prob[j])
        if j & 1 == j >> 1:
            raw[0 if j else 1, part] = product
        else:
            i = 0 if j == DIAGONAL else 1
            send_c[i, part] = (product * mine[1, j]).astype(BF16)
            sum_c(t, i).start()

    def prob_grad(j):
        grads = prob[j].astype(F32) * dot(flat(VALUE), rt[GRAD, j])
        prod[j] = grads.astype(BF16)
        stat[1, OWN, :, j * rows:(j + 1) * rows] = jnp.sum(grads, axis=0, keepdims=True) * mine[1, j]

    gather_y(GRAD).wait_recv()
    forward(GRAD).start()
    for rz in range(1, m):
        gather_z(VALUE, rz).wait_recv()
    prob_grad(OWN)
    prob_grad(SIBLING)
    prob_grad(PARTNER)
    left[:hd] = flat(VALUE).T
    query_side(DIAGONAL, 0)
    forward(GRAD).wait_recv()
    prob_grad(DIAGONAL)
    for j in others:
        share(1, j).start()
    query_side(DIAGONAL, 1)
    query_side(PARTNER, 0)
    query_side(PARTNER, 1)

    def shared(t, r, j):
        return stat[t, r, :, (r ^ j) * rows:((r ^ j) + 1) * rows]

    for j in others:
        share(0, j).wait_recv()
    shares, factors = [], []
    for j in quad:
        parts = [shared(0, r, j) for r in quad]
        top = jnp.maximum(jnp.maximum(parts[0], parts[1]), jnp.maximum(parts[2], parts[3]))
        log_sum = top + jnp.log2(sum(jnp.exp2(part - top) for part in parts))
        shares.append([jnp.exp2(part - log_sum) for part in parts])
        factors.append(jnp.exp2(mine[0, j] - log_sum))

    def key_side(weights, sides, start, stop):
        return sum(dot_t(weights[j, start * tok:stop * tok], sides[j]) for j in quad)

    def send_key_side(t, make):
        for start, stop in ((m // 4, m - m // 4), (m - m // 4, m), (0, m // 4)):
            total = make(start, stop)
            for rz in sorted(range(start, stop), key=lambda r: -min(r, m - r)):
                if rz:
                    send_z[t, rz] = total[(rz - start) * tok:(rz - start + 1) * tok].astype(BF16)
                    sum_z(t, rz).start()
        return total[:tok]

    def both_cores(i, t):
        j = OWN if i else PARTNER
        part = slice(t * hd, (t + 1) * hd)
        return raw[i, part] * factors[j] + recv_c[i, part].astype(F32) * shares[j][SIBLING]

    def out_part(i):
        return both_cores(i, 0)

    def dq_part(i):
        return (both_cores(i, 2) - both_cores(i, 1) * deltas[OWN if i else PARTNER]) * scale

    def pass_query_side(t, part):
        sum_c(t, 0).wait_recv()
        send_y[t] = part(0).astype(BF16)
        sum_y(t).start()

    def finish_query_side(t, total, out_ref):
        sum_y(t).wait_recv()
        total = (total + recv_y[t].astype(F32)).astype(BF16)
        for h in range(heads):
            out_ref[:, h * hd:(h + 1) * hd] = total[:, h * tok:(h + 1) * tok].T

    def finish_key_side(t, total, out_ref, by):
        for rz in reversed(far):
            sum_z(t, rz).wait_recv()
            total = total + recv_z[t, m - rz].astype(F32)
        out_ref[...] = total * by

    pass_query_side(OUT, out_part)
    scaled_grads = [(rt[GRAD, j].astype(F32) * factors[j]).astype(BF16) for j in quad]
    dv = send_key_side(VALUE, lambda start, stop: key_side(prob, scaled_grads, start, stop))
    query_side(SIBLING, 0)
    query_side(SIBLING, 1)
    query_side(OWN, 0)
    query_side(OWN, 1)
    scaled = [rt[QUERY, j].astype(F32) * factors[j] for j in quad]
    first = key_side(prod, [side.astype(BF16) for side in scaled], 0, m)

    for j in others:
        share(1, j).wait_recv()
    deltas = [sum(shared(1, r, j) * shares[j][r] for r in quad) for j in quad]
    pass_query_side(DQ, dq_part)
    lowered = [(side * delta).astype(BF16) for side, delta in zip(scaled, deltas)]
    dk = send_key_side(
        KEY, lambda start, stop: first[start * tok:stop * tok] - key_side(prob, lowered, start, stop)
    )

    for t in (0, 1):
        gather_y(t).wait_send()
        if t == 0:
            gather_c().wait_send()
        forward(t).wait_send()
        for i in (0, 1):
            sum_c(t, i).wait_send()
        for j in others:
            share(t, j).wait_send()
        for rz in range(1, m):
            gather_z(t, rz).wait_send()
    sum_c(OUT, 1).wait_recv()
    finish_query_side(OUT, out_part(1), att_ref)
    finish_key_side(VALUE, dv, dv_ref, 1.0)
    sum_y(OUT).wait_send()
    for rz in far:
        sum_z(VALUE, rz).wait_send()
    sum_c(DQ, 1).wait_recv()
    dq = dq_part(1)
    for rz in far:
        sum_z(KEY, rz).wait_send()
    sum_y(DQ).wait_send()
    finish_key_side(KEY, dk, dk_ref, scale)
    finish_query_side(DQ, dq, dq_ref)


def write_out(*refs):
    out_s = refs[8]
    stores = [pltpu.make_async_copy(refs[i], refs[4 + i], out_s.at[i]) for i in range(4)]
    for store in stores:
        store.start()
    for store in stores:
        store.wait()


def shards(queries, key_states, value_states, grad_out, tile_mask, block_order):
    n = lax.axis_size("blk")
    m = n // 4
    tok, hd = key_states.shape
    rows = queries.shape[1] // hd * tok
    assert n == 4 * m and tile_mask.shape[1] == n
    hbm = pl.BlockSpec(memory_space=pltpu.HBM)
    vmem = pl.BlockSpec(memory_space=pltpu.VMEM)
    dma = pltpu.SemaphoreType.DMA
    shapes = (
        jax.ShapeDtypeStruct(queries.shape, BF16),
        jax.ShapeDtypeStruct(queries.shape, BF16),
        jax.ShapeDtypeStruct(key_states.shape, F32),
        jax.ShapeDtypeStruct(key_states.shape, F32),
    )
    results = pl.pallas_call(
        functools.partial(kernel, n),
        out_shape=tuple(pltpu.VMEM(s.shape, s.dtype) for s in shapes),
        in_specs=[hbm] * 6,
        out_specs=(vmem,) * 4,
        scratch_shapes=[
            pltpu.SMEM(tile_mask.shape, jnp.int32),
            pltpu.SMEM(block_order.shape, jnp.int32),
            pltpu.VMEM(queries.shape, BF16),
            pltpu.VMEM(queries.shape, BF16),
            pltpu.VMEM((2, m, tok, hd), BF16),
            pltpu.VMEM((2, 4, hd, rows), BF16),
            pltpu.VMEM((4, m * tok, rows), BF16),
            pltpu.VMEM((4, m * tok, rows), BF16),
            pltpu.VMEM((2 * hd, m * tok), BF16),
            pltpu.VMEM((2, 3 * hd, rows), F32),
            pltpu.VMEM((2, 4, 1, 4 * rows), F32),
            pltpu.VMEM((2, 4, 1, rows), F32),
            pltpu.VMEM((2, m, tok, hd), BF16),
            pltpu.VMEM((2, m, tok, hd), BF16),
            pltpu.VMEM((2, 3 * hd, rows), BF16),
            pltpu.VMEM((2, 3 * hd, rows), BF16),
            pltpu.VMEM((2, hd, rows), BF16),
            pltpu.VMEM((2, hd, rows), BF16),
            dma((6,)), dma((2, m)), dma((2, m)), dma((2,)), dma((2,)), dma((2,)), dma((2,)), dma((2,)), dma((2,)),
            dma((2, 4)), dma((2, 4)), dma((2, m)), dma((2, m)), dma((2, 2)), dma((2, 2)), dma((2,)), dma((2,)),
        ],
        compiler_params=pltpu.CompilerParams(
            collective_id=0, has_side_effects=True, vmem_limit_bytes=58 * 1024 * 1024
        ),
    )(queries, key_states, value_states, grad_out, tile_mask, block_order)
    return pl.pallas_call(
        write_out,
        out_shape=shapes,
        in_specs=[vmem] * 4,
        out_specs=(hbm,) * 4,
        scratch_shapes=[dma((4,))],
        compiler_params=pltpu.CompilerParams(vmem_limit_bytes=8 * 1024 * 1024),
    )(*results)


def solution(mesh):
    both = P(("groups", "blk"), None)
    return jax.shard_map(
        shards,
        mesh=mesh,
        in_specs=(both, both, both, both, P("groups", None), P("groups")),
        out_specs=(both, both, both, both),
        check_vma=False,
    )
```

```python
import functools
import math

import jax
import jax.numpy as jnp
from jax import lax
from jax.experimental import pallas as pl
from jax.experimental.pallas import tpu as pltpu
from jax.sharding import PartitionSpec as P

MESH = pl.DeviceIdType.MESH
F32 = jnp.float32
BF16 = jnp.bfloat16
MASKED = -1e30


def dot(a, b):
    return jnp.dot(a, b, preferred_element_type=F32)


def dot_t(a, b):
    return lax.dot_general(a, b, (((1,), (1,)), ((), ())), preferred_element_type=F32)


def kernel(
    n, q_hbm, k_hbm, v_hbm, g_hbm, mask_hbm, order_hbm, att_ref, dq_ref, dk_ref, dv_ref,
    mask_ref, order_ref, q_ref, g_ref, kv, rt, prob, prod, left, raw, stat, mine, send_z, recv_z, send_c, recv_c, send_y, recv_y,
    in_s, z_s, z_r, y_s, y_r, c_s, c_r, f_s, f_r, t_s, t_r, gz_s, gz_r, gc_s, gc_r, gy_s, gy_r,
):
    m = n // 4
    tok, hd = k_hbm.shape
    heads = q_hbm.shape[1] // hd
    rows = heads * tok
    keys = m * tok
    scale = hd ** -0.5
    to_exp2 = scale * math.log2(math.e)
    KEY, VALUE = 0, 1
    QUERY, GRAD = 0, 1
    OUT, DQ = 0, 1
    OWN, SIBLING, DIAGONAL, PARTNER = 0, 1, 2, 3
    quad = (OWN, SIBLING, DIAGONAL, PARTNER)
    others = (DIAGONAL, PARTNER, SIBLING)

    me = lax.axis_index("blk")
    z, y, c = me // 4, (me // 2) % 2, me % 2

    def index(rz, j):
        zz = lax.rem(z + rz, m)
        yy = 1 - y if j & 2 else y
        cc = 1 - c if j & 1 else c
        return (zz * 2 + yy) * 2 + cc

    def chunk(rz):
        return index(rz, 1 if rz else 0)

    def remote(src, dst, s_sem, r_sem, target):
        return pltpu.make_async_remote_copy(
            src_ref=src, dst_ref=dst, send_sem=s_sem, recv_sem=r_sem,
            device_id={"blk": target}, device_id_type=MESH,
        )

    def gather_z(t, g):
        return remote(kv.at[t, 0], kv.at[t, m - g], z_s.at[t, g], z_r.at[t, m - g], chunk(g))

    def gather_y(t):
        return remote(rt.at[t, OWN], rt.at[t, PARTNER], y_s.at[t], y_r.at[t], index(0, PARTNER))

    def gather_c():
        return remote(rt.at[:, OWN], rt.at[:, SIBLING], c_s.at[0], c_r.at[0], index(0, SIBLING))

    def forward(t):
        return remote(rt.at[t, PARTNER], rt.at[t, DIAGONAL], f_s.at[t], f_r.at[t], index(0, SIBLING))

    def share(t, j):
        return remote(stat.at[t, OWN], stat.at[t, j], t_s.at[t, j], t_r.at[t, j], index(0, j))

    def sum_z(t, rz):
        return remote(send_z.at[t, rz], recv_z.at[t, m - rz], gz_s.at[t, rz], gz_r.at[t, m - rz], chunk(rz))

    def sum_c(t, i):
        part = pl.ds(2 * hd, hd) if t else pl.ds(0, 2 * hd)
        return remote(send_c.at[i, part], recv_c.at[i, part], gc_s.at[t, i], gc_r.at[t, i], index(0, SIBLING))

    def sum_y(t):
        return remote(send_y.at[t], recv_y.at[t], gy_s.at[t], gy_r.at[t], index(0, PARTNER))

    barrier = pltpu.get_barrier_semaphore()
    for other in [chunk(g) for g in range(1, m)] + [index(0, j) for j in others]:
        pl.semaphore_signal(barrier, inc=1, device_id={"blk": other}, device_id_type=MESH)
    loads = [
        pltpu.make_async_copy(src, dst, in_s.at[i])
        for i, (src, dst) in enumerate(
            [(q_hbm, q_ref), (g_hbm, g_ref), (k_hbm, kv.at[KEY, 0]), (v_hbm, kv.at[VALUE, 0]),
             (mask_hbm, mask_ref), (order_hbm, order_ref)]
        )
    ]
    for load in loads:
        load.start()
    far = sorted(range(1, m), key=lambda r: -min(r, m - r))
    def turn(t, ref):
        loads[t].wait()
        for h in range(heads):
            rt[t, OWN, :, h * tok:(h + 1) * tok] = ref[:, h * hd:(h + 1) * hd].T

    turn(QUERY, q_ref)
    turn(GRAD, g_ref)
    for load in loads[2:]:
        load.wait()
    pl.semaphore_wait(barrier, m + 2)
    gather_y(QUERY).start()
    for rz in far:
        gather_z(KEY, rz).start()
    gather_y(GRAD).start()
    gather_c().start()
    for rz in far:
        gather_z(VALUE, rz).start()

    blocks = [order_ref[index(0, j)] for j in quad]
    key_ids = lax.broadcasted_iota(jnp.int32, (tok, rows), 0)
    row_ids = lax.broadcasted_iota(jnp.int32, (tok, rows), 1) % tok
    causal = jnp.where(row_ids >= key_ids, 0.0, MASKED).astype(F32)

    def bias(j, rz):
        if rz == 0 and j == OWN:
            return causal
        block = order_ref[chunk(rz)]
        seen = (blocks[j] > block) & (mask_ref[blocks[j], block] == 1)
        return jnp.where(seen, 0.0, MASKED).astype(F32)

    def flat(t):
        return kv[t].reshape(keys, hd)

    def score(j):
        scores = dot(flat(KEY), rt[QUERY, j])
        top = jnp.full((1, rows), 0.1 * MASKED, F32)
        parts = []
        for rz in range(m):
            s = scores[rz * tok:(rz + 1) * tok]
            b = bias(j, rz)
            if rz == 0 and j == OWN:
                s = s * to_exp2 + b
                top = jnp.maximum(top, jnp.max(s, axis=0, keepdims=True))
            else:
                top = jnp.maximum(top, jnp.max(s, axis=0, keepdims=True) * to_exp2 + b)
            parts.append((s, b))
        total = jnp.zeros((1, rows), F32)
        for rz, (s, b) in enumerate(parts):
            if rz == 0 and j == OWN:
                p = jnp.exp2(s - top)
            else:
                p = jnp.exp2(s * to_exp2 + (b - top))
            total = total + jnp.sum(p, axis=0, keepdims=True)
            prob[j, rz * tok:(rz + 1) * tok, :] = p.astype(BF16)
        log_sum = top + jnp.log2(jnp.maximum(total, 1e-37))
        mine[0, j] = top
        mine[1, j] = jnp.exp2(top - log_sum)
        stat[0, OWN, :, j * rows:(j + 1) * rows] = log_sum

    gather_y(QUERY).wait_recv()
    forward(QUERY).start()
    for rz in range(1, m):
        gather_z(KEY, rz).wait_recv()
    score(OWN)
    gather_c().wait_recv()
    score(SIBLING)
    score(PARTNER)
    forward(QUERY).wait_recv()
    score(DIAGONAL)
    for j in others:
        share(0, j).start()
    left[hd:] = flat(KEY).T

    def query_side(j, t):
        part = slice(2 * hd, 3 * hd) if t else slice(0, 2 * hd)
        product = dot(left[hd:], prod[j]) if t else dot(left[...], prob[j])
        if j & 1 == j >> 1:
            raw[0 if j else 1, part] = product
        else:
            i = 0 if j == DIAGONAL else 1
            send_c[i, part] = (product * mine[1, j]).astype(BF16)
            sum_c(t, i).start()

    def prob_grad(j):
        grads = prob[j].astype(F32) * dot(flat(VALUE), rt[GRAD, j])
        prod[j] = grads.astype(BF16)
        stat[1, OWN, :, j * rows:(j + 1) * rows] = jnp.sum(grads, axis=0, keepdims=True) * mine[1, j]

    gather_y(GRAD).wait_recv()
    forward(GRAD).start()
    for rz in range(1, m):
        gather_z(VALUE, rz).wait_recv()
    prob_grad(OWN)
    prob_grad(SIBLING)
    prob_grad(PARTNER)
    left[:hd] = flat(VALUE).T
    query_side(DIAGONAL, 0)
    forward(GRAD).wait_recv()
    prob_grad(DIAGONAL)
    for j in others:
        share(1, j).start()
    query_side(DIAGONAL, 1)
    query_side(PARTNER, 0)
    query_side(PARTNER, 1)

    def shared(t, r, j):
        return stat[t, r, :, (r ^ j) * rows:((r ^ j) + 1) * rows]

    for j in others:
        share(0, j).wait_recv()
    shares, factors = [], []
    for j in quad:
        parts = [shared(0, r, j) for r in quad]
        top = jnp.maximum(jnp.maximum(parts[0], parts[1]), jnp.maximum(parts[2], parts[3]))
        log_sum = top + jnp.log2(sum(jnp.exp2(part - top) for part in parts))
        shares.append([jnp.exp2(part - log_sum) for part in parts])
        factors.append(jnp.exp2(mine[0, j] - log_sum))

    def key_side(weights, sides, start, stop):
        return sum(dot_t(weights[j, start * tok:stop * tok], sides[j]) for j in quad)

    def send_key_side(t, make):
        for start, stop in [(rz, rz + 1) for rz in far + [0]]:
            total = make(start, stop)
            for rz in sorted(range(start, stop), key=lambda r: -min(r, m - r)):
                if rz:
                    send_z[t, rz] = total[(rz - start) * tok:(rz - start + 1) * tok].astype(BF16)
                    sum_z(t, rz).start()
        return total[:tok]

    def both_cores(i, t):
        j = OWN if i else PARTNER
        part = slice(t * hd, (t + 1) * hd)
        return raw[i, part] * factors[j] + recv_c[i, part].astype(F32) * shares[j][SIBLING]

    def out_part(i):
        return both_cores(i, 0)

    def dq_part(i):
        return (both_cores(i, 2) - both_cores(i, 1) * deltas[OWN if i else PARTNER]) * scale

    def pass_query_side(t, part):
        sum_c(t, 0).wait_recv()
        send_y[t] = part(0).astype(BF16)
        sum_y(t).start()

    def finish_query_side(t, total, out_ref):
        sum_y(t).wait_recv()
        total = (total + recv_y[t].astype(F32)).astype(BF16)
        for h in range(heads):
            out_ref[:, h * hd:(h + 1) * hd] = total[:, h * tok:(h + 1) * tok].T

    def finish_key_side(t, total, out_ref, by):
        for rz in reversed(far):
            sum_z(t, rz).wait_recv()
            total = total + recv_z[t, m - rz].astype(F32)
        out_ref[...] = total * by

    pass_query_side(OUT, out_part)
    scaled_grads = [(rt[GRAD, j].astype(F32) * factors[j]).astype(BF16) for j in quad]
    dv = send_key_side(VALUE, lambda start, stop: key_side(prob, scaled_grads, start, stop))
    query_side(SIBLING, 0)
    query_side(SIBLING, 1)
    query_side(OWN, 0)
    query_side(OWN, 1)
    scaled = [rt[QUERY, j].astype(F32) * factors[j] for j in quad]
    first = key_side(prod, [side.astype(BF16) for side in scaled], 0, m)

    for j in others:
        share(1, j).wait_recv()
    deltas = [sum(shared(1, r, j) * shares[j][r] for r in quad) for j in quad]
    pass_query_side(DQ, dq_part)
    lowered = [(side * delta).astype(BF16) for side, delta in zip(scaled, deltas)]
    dk = send_key_side(
        KEY, lambda start, stop: first[start * tok:stop * tok] - key_side(prob, lowered, start, stop)
    )

    for t in (0, 1):
        gather_y(t).wait_send()
        if t == 0:
            gather_c().wait_send()
        forward(t).wait_send()
        for i in (0, 1):
            sum_c(t, i).wait_send()
        for j in others:
            share(t, j).wait_send()
        for rz in range(1, m):
            gather_z(t, rz).wait_send()
    sum_c(OUT, 1).wait_recv()
    finish_query_side(OUT, out_part(1), att_ref)
    finish_key_side(VALUE, dv, dv_ref, 1.0)
    sum_y(OUT).wait_send()
    for rz in far:
        sum_z(VALUE, rz).wait_send()
    sum_c(DQ, 1).wait_recv()
    dq = dq_part(1)
    finish_query_side(DQ, dq, dq_ref)
    finish_key_side(KEY, dk, dk_ref, scale)
    for rz in far:
        sum_z(KEY, rz).wait_send()
    sum_y(DQ).wait_send()


def write_out(*refs):
    out_s = refs[8]
    stores = [pltpu.make_async_copy(refs[i], refs[4 + i], out_s.at[i]) for i in range(4)]
    for store in stores:
        store.start()
    for store in stores:
        store.wait()


def shards(queries, key_states, value_states, grad_out, tile_mask, block_order):
    n = lax.axis_size("blk")
    m = n // 4
    tok, hd = key_states.shape
    rows = queries.shape[1] // hd * tok
    assert n == 4 * m and tile_mask.shape[1] == n
    hbm = pl.BlockSpec(memory_space=pltpu.HBM)
    vmem = pl.BlockSpec(memory_space=pltpu.VMEM)
    dma = pltpu.SemaphoreType.DMA
    shapes = (
        jax.ShapeDtypeStruct(queries.shape, BF16),
        jax.ShapeDtypeStruct(queries.shape, BF16),
        jax.ShapeDtypeStruct(key_states.shape, F32),
        jax.ShapeDtypeStruct(key_states.shape, F32),
    )
    results = pl.pallas_call(
        functools.partial(kernel, n),
        out_shape=tuple(pltpu.VMEM(s.shape, s.dtype) for s in shapes),
        in_specs=[hbm] * 6,
        out_specs=(vmem,) * 4,
        scratch_shapes=[
            pltpu.SMEM(tile_mask.shape, jnp.int32),
            pltpu.SMEM(block_order.shape, jnp.int32),
            pltpu.VMEM(queries.shape, BF16),
            pltpu.VMEM(queries.shape, BF16),
            pltpu.VMEM((2, m, tok, hd), BF16),
            pltpu.VMEM((2, 4, hd, rows), BF16),
            pltpu.VMEM((4, m * tok, rows), BF16),
            pltpu.VMEM((4, m * tok, rows), BF16),
            pltpu.VMEM((2 * hd, m * tok), BF16),
            pltpu.VMEM((2, 3 * hd, rows), F32),
            pltpu.VMEM((2, 4, 1, 4 * rows), F32),
            pltpu.VMEM((2, 4, 1, rows), F32),
            pltpu.VMEM((2, m, tok, hd), BF16),
            pltpu.VMEM((2, m, tok, hd), BF16),
            pltpu.VMEM((2, 3 * hd, rows), BF16),
            pltpu.VMEM((2, 3 * hd, rows), BF16),
            pltpu.VMEM((2, hd, rows), BF16),
            pltpu.VMEM((2, hd, rows), BF16),
            dma((6,)), dma((2, m)), dma((2, m)), dma((2,)), dma((2,)), dma((2,)), dma((2,)), dma((2,)), dma((2,)),
            dma((2, 4)), dma((2, 4)), dma((2, m)), dma((2, m)), dma((2, 2)), dma((2, 2)), dma((2,)), dma((2,)),
        ],
        compiler_params=pltpu.CompilerParams(
            collective_id=0, has_side_effects=True, vmem_limit_bytes=58 * 1024 * 1024
        ),
    )(queries, key_states, value_states, grad_out, tile_mask, block_order)
    return pl.pallas_call(
        write_out,
        out_shape=shapes,
        in_specs=[vmem] * 4,
        out_specs=(hbm,) * 4,
        scratch_shapes=[dma((4,))],
        compiler_params=pltpu.CompilerParams(vmem_limit_bytes=8 * 1024 * 1024),
    )(*results)


def solution(mesh):
    both = P(("groups", "blk"), None)
    return jax.shard_map(
        shards,
        mesh=mesh,
        in_specs=(both, both, both, both, P("groups", None), P("groups")),
        out_specs=(both, both, both, both),
        check_vma=False,
    )
```

```python
import functools
import math

import jax
import jax.numpy as jnp
from jax import lax
from jax.experimental import pallas as pl
from jax.experimental.pallas import tpu as pltpu
from jax.sharding import PartitionSpec as P

MESH = pl.DeviceIdType.MESH
F32 = jnp.float32
BF16 = jnp.bfloat16
MASKED = -1e30


def dot(a, b):
    return jnp.dot(a, b, preferred_element_type=F32)


def dot_t(a, b):
    return lax.dot_general(a, b, (((1,), (1,)), ((), ())), preferred_element_type=F32)


def kernel(
    n, q_hbm, k_hbm, v_hbm, g_hbm, mask_hbm, order_hbm, att_ref, dq_ref, dk_ref, dv_ref,
    mask_ref, order_ref, q_ref, g_ref, kv, rt, prob, prod, left, raw, stat, mine, send_z, recv_z, send_c, recv_c, send_y, recv_y,
    in_s, z_s, z_r, y_s, y_r, c_s, c_r, f_s, f_r, t_s, t_r, gz_s, gz_r, gc_s, gc_r, gy_s, gy_r,
):
    m = n // 4
    tok, hd = k_hbm.shape
    heads = q_hbm.shape[1] // hd
    rows = heads * tok
    keys = m * tok
    scale = hd ** -0.5
    to_exp2 = scale * math.log2(math.e)
    KEY, VALUE = 0, 1
    QUERY, GRAD = 0, 1
    OUT, DQ = 0, 1
    OWN, SIBLING, DIAGONAL, PARTNER = 0, 1, 2, 3
    quad = (OWN, SIBLING, DIAGONAL, PARTNER)
    others = (PARTNER, SIBLING, DIAGONAL)

    me = lax.axis_index("blk")
    z, y, c = me // 4, (me // 2) % 2, me % 2

    def index(rz, j):
        zz = lax.rem(z + rz, m)
        yy = 1 - y if j & 2 else y
        cc = 1 - c if j & 1 else c
        return (zz * 2 + yy) * 2 + cc

    def chunk(rz):
        return index(rz, 1 if rz else 0)

    def remote(src, dst, s_sem, r_sem, target):
        return pltpu.make_async_remote_copy(
            src_ref=src, dst_ref=dst, send_sem=s_sem, recv_sem=r_sem,
            device_id={"blk": target}, device_id_type=MESH,
        )

    def gather_z(t, g):
        return remote(kv.at[t, 0], kv.at[t, m - g], z_s.at[t, g], z_r.at[t, m - g], chunk(g))

    def gather_y(t):
        return remote(rt.at[t, OWN], rt.at[t, PARTNER], y_s.at[t], y_r.at[t], index(0, PARTNER))

    def gather_c():
        return remote(rt.at[:, OWN], rt.at[:, SIBLING], c_s.at[0], c_r.at[0], index(0, SIBLING))

    def forward(t):
        return remote(rt.at[t, PARTNER], rt.at[t, DIAGONAL], f_s.at[t], f_r.at[t], index(0, SIBLING))

    def share(t, j):
        return remote(stat.at[t, OWN], stat.at[t, j], t_s.at[t, j], t_r.at[t, j], index(0, j))

    def sum_z(t, rz):
        return remote(send_z.at[t, rz], recv_z.at[t, m - rz], gz_s.at[t, rz], gz_r.at[t, m - rz], chunk(rz))

    def sum_c(t, i):
        part = pl.ds(2 * hd, hd) if t else pl.ds(0, 2 * hd)
        return remote(send_c.at[i, part], recv_c.at[i, part], gc_s.at[t, i], gc_r.at[t, i], index(0, SIBLING))

    def sum_y(t):
        return remote(send_y.at[t], recv_y.at[t], gy_s.at[t], gy_r.at[t], index(0, PARTNER))

    barrier = pltpu.get_barrier_semaphore()
    for other in [chunk(g) for g in range(1, m)] + [index(0, j) for j in others]:
        pl.semaphore_signal(barrier, inc=1, device_id={"blk": other}, device_id_type=MESH)
    loads = [
        pltpu.make_async_copy(src, dst, in_s.at[i])
        for i, (src, dst) in enumerate(
            [(q_hbm, q_ref), (g_hbm, g_ref), (k_hbm, kv.at[KEY, 0]), (v_hbm, kv.at[VALUE, 0]),
             (mask_hbm, mask_ref), (order_hbm, order_ref)]
        )
    ]
    for load in loads:
        load.start()
    far = sorted(range(1, m), key=lambda r: -min(r, m - r))
    def turn(t, ref):
        loads[t].wait()
        for h in range(heads):
            rt[t, OWN, :, h * tok:(h + 1) * tok] = ref[:, h * hd:(h + 1) * hd].T

    turn(QUERY, q_ref)
    turn(GRAD, g_ref)
    for load in loads[2:]:
        load.wait()
    pl.semaphore_wait(barrier, m + 2)
    gather_y(QUERY).start()
    for rz in far:
        gather_z(KEY, rz).start()
    gather_y(GRAD).start()
    gather_c().start()
    for rz in far:
        gather_z(VALUE, rz).start()

    blocks = [order_ref[index(0, j)] for j in quad]
    key_ids = lax.broadcasted_iota(jnp.int32, (tok, rows), 0)
    row_ids = lax.broadcasted_iota(jnp.int32, (tok, rows), 1) % tok
    causal = jnp.where(row_ids >= key_ids, 0.0, MASKED).astype(F32)

    def bias(j, rz):
        if rz == 0 and j == OWN:
            return causal
        block = order_ref[chunk(rz)]
        seen = (blocks[j] > block) & (mask_ref[blocks[j], block] == 1)
        return jnp.where(seen, 0.0, MASKED).astype(F32)

    def flat(t):
        return kv[t].reshape(keys, hd)

    def score(j):
        scores = dot(flat(KEY), rt[QUERY, j])
        top = jnp.full((1, rows), 0.1 * MASKED, F32)
        parts = []
        for rz in range(m):
            s = scores[rz * tok:(rz + 1) * tok]
            b = bias(j, rz)
            if rz == 0 and j == OWN:
                s = s * to_exp2 + b
                top = jnp.maximum(top, jnp.max(s, axis=0, keepdims=True))
            else:
                top = jnp.maximum(top, jnp.max(s, axis=0, keepdims=True) * to_exp2 + b)
            parts.append((s, b))
        total = jnp.zeros((1, rows), F32)
        for rz, (s, b) in enumerate(parts):
            if rz == 0 and j == OWN:
                p = jnp.exp2(s - top)
            else:
                p = jnp.exp2(s * to_exp2 + (b - top))
            total = total + jnp.sum(p, axis=0, keepdims=True)
            prob[j, rz * tok:(rz + 1) * tok, :] = p.astype(BF16)
        log_sum = top + jnp.log2(jnp.maximum(total, 1e-37))
        mine[0, j] = top
        mine[1, j] = jnp.exp2(top - log_sum)
        stat[0, OWN, :, j * rows:(j + 1) * rows] = log_sum

    gather_y(QUERY).wait_recv()
    forward(QUERY).start()
    for rz in range(1, m):
        gather_z(KEY, rz).wait_recv()
    score(OWN)
    gather_c().wait_recv()
    score(SIBLING)
    score(PARTNER)
    forward(QUERY).wait_recv()
    score(DIAGONAL)
    for j in others:
        share(0, j).start()
    left[hd:] = flat(KEY).T

    def query_side(j, t):
        part = slice(2 * hd, 3 * hd) if t else slice(0, 2 * hd)
        product = dot(left[hd:], prod[j]) if t else dot(left[...], prob[j])
        if j & 1 == j >> 1:
            raw[0 if j else 1, part] = product
        else:
            i = 0 if j == DIAGONAL else 1
            send_c[i, part] = (product * mine[1, j]).astype(BF16)
            sum_c(t, i).start()

    def prob_grad(j):
        grads = prob[j].astype(F32) * dot(flat(VALUE), rt[GRAD, j])
        prod[j] = grads.astype(BF16)
        stat[1, OWN, :, j * rows:(j + 1) * rows] = jnp.sum(grads, axis=0, keepdims=True) * mine[1, j]

    gather_y(GRAD).wait_recv()
    forward(GRAD).start()
    for rz in range(1, m):
        gather_z(VALUE, rz).wait_recv()
    prob_grad(OWN)
    prob_grad(SIBLING)
    prob_grad(PARTNER)
    left[:hd] = flat(VALUE).T
    query_side(DIAGONAL, 0)
    forward(GRAD).wait_recv()
    prob_grad(DIAGONAL)
    for j in others:
        share(1, j).start()
    query_side(DIAGONAL, 1)
    query_side(PARTNER, 0)
    query_side(PARTNER, 1)

    def shared(t, r, j):
        return stat[t, r, :, (r ^ j) * rows:((r ^ j) + 1) * rows]

    for j in others:
        share(0, j).wait_recv()
    shares, factors = [], []
    for j in quad:
        parts = [shared(0, r, j) for r in quad]
        top = jnp.maximum(jnp.maximum(parts[0], parts[1]), jnp.maximum(parts[2], parts[3]))
        log_sum = top + jnp.log2(sum(jnp.exp2(part - top) for part in parts))
        shares.append([jnp.exp2(part - log_sum) for part in parts])
        factors.append(jnp.exp2(mine[0, j] - log_sum))

    def key_side(weights, sides, start, stop):
        return sum(dot_t(weights[j, start * tok:stop * tok], sides[j]) for j in quad)

    def send_key_side(t, make):
        for start, stop in [(rz, rz + 1) for rz in far + [0]]:
            total = make(start, stop)
            for rz in sorted(range(start, stop), key=lambda r: -min(r, m - r)):
                if rz:
                    send_z[t, rz] = total[(rz - start) * tok:(rz - start + 1) * tok].astype(BF16)
                    sum_z(t, rz).start()
        return total[:tok]

    def both_cores(i, t):
        j = OWN if i else PARTNER
        part = slice(t * hd, (t + 1) * hd)
        return raw[i, part] * factors[j] + recv_c[i, part].astype(F32) * shares[j][SIBLING]

    def out_part(i):
        return both_cores(i, 0)

    def dq_part(i):
        return (both_cores(i, 2) - both_cores(i, 1) * deltas[OWN if i else PARTNER]) * scale

    def pass_query_side(t, part):
        sum_c(t, 0).wait_recv()
        send_y[t] = part(0).astype(BF16)
        sum_y(t).start()

    def finish_query_side(t, total, out_ref):
        sum_y(t).wait_recv()
        total = (total + recv_y[t].astype(F32)).astype(BF16)
        for h in range(heads):
            out_ref[:, h * hd:(h + 1) * hd] = total[:, h * tok:(h + 1) * tok].T

    def finish_key_side(t, total, out_ref, by):
        for rz in reversed(far):
            sum_z(t, rz).wait_recv()
            total = total + recv_z[t, m - rz].astype(F32)
        out_ref[...] = total * by

    pass_query_side(OUT, out_part)
    scaled_grads = [(rt[GRAD, j].astype(F32) * factors[j]).astype(BF16) for j in quad]
    dv = send_key_side(VALUE, lambda start, stop: key_side(prob, scaled_grads, start, stop))
    query_side(SIBLING, 0)
    query_side(SIBLING, 1)
    query_side(OWN, 0)
    query_side(OWN, 1)
    scaled = [rt[QUERY, j].astype(F32) * factors[j] for j in quad]
    first = key_side(prod, [side.astype(BF16) for side in scaled], 0, m)

    for j in others:
        share(1, j).wait_recv()
    deltas = [sum(shared(1, r, j) * shares[j][r] for r in quad) for j in quad]
    pass_query_side(DQ, dq_part)
    lowered = [(side * delta).astype(BF16) for side, delta in zip(scaled, deltas)]
    dk = send_key_side(
        KEY, lambda start, stop: first[start * tok:stop * tok] - key_side(prob, lowered, start, stop)
    )

    for t in (0, 1):
        gather_y(t).wait_send()
        if t == 0:
            gather_c().wait_send()
        forward(t).wait_send()
        for i in (0, 1):
            sum_c(t, i).wait_send()
        for j in others:
            share(t, j).wait_send()
        for rz in range(1, m):
            gather_z(t, rz).wait_send()
    sum_c(OUT, 1).wait_recv()
    finish_query_side(OUT, out_part(1), att_ref)
    finish_key_side(VALUE, dv, dv_ref, 1.0)
    sum_y(OUT).wait_send()
    for rz in far:
        sum_z(VALUE, rz).wait_send()
    sum_c(DQ, 1).wait_recv()
    dq = dq_part(1)
    finish_query_side(DQ, dq, dq_ref)
    finish_key_side(KEY, dk, dk_ref, scale)
    for rz in far:
        sum_z(KEY, rz).wait_send()
    sum_y(DQ).wait_send()


def write_out(*refs):
    out_s = refs[8]
    stores = [pltpu.make_async_copy(refs[i], refs[4 + i], out_s.at[i]) for i in range(4)]
    for store in stores:
        store.start()
    for store in stores:
        store.wait()


def shards(queries, key_states, value_states, grad_out, tile_mask, block_order):
    n = lax.axis_size("blk")
    m = n // 4
    tok, hd = key_states.shape
    rows = queries.shape[1] // hd * tok
    assert n == 4 * m and tile_mask.shape[1] == n
    hbm = pl.BlockSpec(memory_space=pltpu.HBM)
    vmem = pl.BlockSpec(memory_space=pltpu.VMEM)
    dma = pltpu.SemaphoreType.DMA
    shapes = (
        jax.ShapeDtypeStruct(queries.shape, BF16),
        jax.ShapeDtypeStruct(queries.shape, BF16),
        jax.ShapeDtypeStruct(key_states.shape, F32),
        jax.ShapeDtypeStruct(key_states.shape, F32),
    )
    results = pl.pallas_call(
        functools.partial(kernel, n),
        out_shape=tuple(pltpu.VMEM(s.shape, s.dtype) for s in shapes),
        in_specs=[hbm] * 6,
        out_specs=(vmem,) * 4,
        scratch_shapes=[
            pltpu.SMEM(tile_mask.shape, jnp.int32),
            pltpu.SMEM(block_order.shape, jnp.int32),
            pltpu.VMEM(queries.shape, BF16),
            pltpu.VMEM(queries.shape, BF16),
            pltpu.VMEM((2, m, tok, hd), BF16),
            pltpu.VMEM((2, 4, hd, rows), BF16),
            pltpu.VMEM((4, m * tok, rows), BF16),
            pltpu.VMEM((4, m * tok, rows), BF16),
            pltpu.VMEM((2 * hd, m * tok), BF16),
            pltpu.VMEM((2, 3 * hd, rows), F32),
            pltpu.VMEM((2, 4, 1, 4 * rows), F32),
            pltpu.VMEM((2, 4, 1, rows), F32),
            pltpu.VMEM((2, m, tok, hd), BF16),
            pltpu.VMEM((2, m, tok, hd), BF16),
            pltpu.VMEM((2, 3 * hd, rows), BF16),
            pltpu.VMEM((2, 3 * hd, rows), BF16),
            pltpu.VMEM((2, hd, rows), BF16),
            pltpu.VMEM((2, hd, rows), BF16),
            dma((6,)), dma((2, m)), dma((2, m)), dma((2,)), dma((2,)), dma((2,)), dma((2,)), dma((2,)), dma((2,)),
            dma((2, 4)), dma((2, 4)), dma((2, m)), dma((2, m)), dma((2, 2)), dma((2, 2)), dma((2,)), dma((2,)),
        ],
        compiler_params=pltpu.CompilerParams(
            collective_id=0, has_side_effects=True, vmem_limit_bytes=58 * 1024 * 1024
        ),
    )(queries, key_states, value_states, grad_out, tile_mask, block_order)
    return pl.pallas_call(
        write_out,
        out_shape=shapes,
        in_specs=[vmem] * 4,
        out_specs=(hbm,) * 4,
        scratch_shapes=[dma((4,))],
        compiler_params=pltpu.CompilerParams(vmem_limit_bytes=8 * 1024 * 1024),
    )(*results)


def solution(mesh):
    both = P(("groups", "blk"), None)
    return jax.shard_map(
        shards,
        mesh=mesh,
        in_specs=(both, both, both, both, P("groups", None), P("groups")),
        out_specs=(both, both, both, both),
        check_vma=False,
    )
```
